512 devices in a mesh: band: 4 (over z_hi, core), dom: 128 (over y, x, z_lo).
Axes of the slice: x: 4, y: 8, z: 8 (z_hi: 2, z_lo: 4; z = z_hi * 4 + z_lo), core: 2. Of those that a mesh axis runs over, the one named last changes fastest.
Arguments:
- orbitals: float32 [128, 8, 12, 16, 512], P('dom', None, None, None, 'band'), may hold values from -8 to 8, as said below
- potential: float32 [128, 8, 12, 16], P('dom'), may hold values from -2 to 0.5
- bounds: float32 [3], replicated, may hold values from -2.6 to 36, as said below
- rotation: float32 [512, 512], P(None, 'band'), may hold values from -0.2 to 1.2
Outputs:
- rotated: float32 [128, 8, 12, 16, 512], P('dom', None, None, None, 'band')
- margin: float32 [512, 512], P(None, 'band')
- projected: float32 [512, 512], P(None, 'band')
The draws below stay inside these ranges and needn't reach their ends.
Inputs may be any that keep to these rules, and one draw needn't show every extreme that they name: `orbitals`: amplitudes vary smoothly in size across the grid. bounds holds the lowest-eigenvalue estimate, the cutoff and a bound above the largest eigenvalue of H, in that order.
All inputs are finite; a program needn't handle non-finite values.
Results may differ from the reference program's by a relative error of at most 0.0001.
Values sent between devices are 32-bit elements; how exact they have to be, the bound alone decides.
No kernel may reach another device: no remote copies, remote signals or barrier semaphores. Data moves between devices by JAX's collectives and lax.ppermute only.
A program may use at most 64 MiB of HBM per device.

```python
import jax
import jax.numpy as jnp
from jax import lax

BX = 8
BY = 12
BZ = 16
BANDS = 512
DEGREE = 3
PZ = 8
PY = 4
PX = 4
BLOCKS = 128
NX = 32
NY = 48
NZ = 128
N_BAND = 4


def draw_orbitals(key, part):
    key = jax.random.fold_in(key, 11)
    full_shape = (BLOCKS, BX, BY, BZ, BANDS)
    block_ids = lax.broadcasted_iota(jnp.int32, full_shape[:4], 0)
    local_x = lax.broadcasted_iota(jnp.int32, full_shape[:4], 1)
    global_x = block_ids // (PY * PZ) * BX + local_x
    fraction = global_x.astype(jnp.float32) / NX
    base_draw = jnp.clip(jax.random.normal(key, full_shape, jnp.float32), -5.0, 5.0)
    rising = 0.5 + fraction
    return base_draw * rising[..., None]


def draw_bounds(key, part):
    key = jax.random.fold_in(key, 12)
    uniforms = jax.random.uniform(key, (3,), jnp.float32)
    lowest = -2.6 + 0.4 * uniforms[0]
    cutoff = 1.5 + 1.5 * uniforms[1]
    highest = 31.0 + 5.0 * uniforms[2]
    return jnp.stack([lowest, cutoff, highest]).astype(jnp.float32)


def draw_rotation(key, part):
    key = jax.random.fold_in(key, 13)
    rows = lax.broadcasted_iota(jnp.int32, (BANDS, BANDS), 0)
    columns = lax.broadcasted_iota(jnp.int32, (BANDS, BANDS), 1)
    identity = jnp.where(rows == columns, 1.0, 0.0).astype(jnp.float32)
    spread = jnp.clip(jax.random.normal(key, (BANDS, BANDS), jnp.float32), -5.0, 5.0)
    return identity + 0.5 / BANDS ** 0.5 * spread


def shard_levels(own_key, extent, shards, least, largest):
    def one(axis_at, shards_of):
        heights = jax.random.uniform(jax.random.fold_in(jax.random.fold_in(own_key, 6), axis_at), (shards_of,), jnp.float32, least / len(shards), largest / len(shards))
        return jnp.repeat(jnp.exp(heights), extent[axis_at] // shards_of).reshape((-1,) + (1,) * (len(extent) - axis_at - 1))

    gain = one(*shards[0])
    for cut in shards[1:]:
        gain = gain * one(*cut)
    return gain


def setup_inputs(seed: int = 0) -> dict:
    arg_keys = jax.random.split(jax.random.key(seed), 5)
    orbitals = draw_orbitals(jax.random.fold_in(arg_keys[4], 71), 0)
    potential = jnp.clip(-2.0 + 2.5 * jax.random.uniform(arg_keys[1], (BLOCKS, BX, BY, BZ), jnp.float32) ** shard_levels(arg_keys[1], (BLOCKS, BX, BY, BZ), ((0, 128),), -0.2, 0.2), -2.0, 0.5)
    bounds = draw_bounds(jax.random.fold_in(arg_keys[4], 71), 0)
    rotation = draw_rotation(jax.random.fold_in(arg_keys[4], 71), 0)
    return {"orbitals": orbitals, "potential": potential, "bounds": bounds, "rotation": rotation}


STENCIL = (-5369.0 / 1800.0, 12.0 / 7.0, -15.0 / 56.0, 10.0 / 189.0, -1.0 / 112.0, 2.0 / 1925.0, -1.0 / 16632.0)
INV_SPACING2 = 1.0 / 0.36

def laplace_grid(values):
    stencil_reach = len(STENCIL) - 1
    summed = 3.0 * STENCIL[0] * values
    for dim_index in range(3):
        widths = [(0, 0)] * values.ndim
        widths[dim_index] = (stencil_reach, stencil_reach)
        padded = jnp.pad(values, widths)
        length = values.shape[dim_index]
        for offset in range(1, stencil_reach + 1):
            upper_part = lax.slice_in_dim(padded, stencil_reach + offset, stencil_reach + offset + length, axis=dim_index)
            lower_part = lax.slice_in_dim(padded, stencil_reach - offset, stencil_reach - offset + length, axis=dim_index)
            summed = summed + STENCIL[offset] * (upper_part + lower_part)
    return summed

def hamiltonian(values, potential_grid):
    return -0.5 * INV_SPACING2 * laplace_grid(values) + potential_grid[..., None] * values

def chebyshev(start_block, operator_fn, bounds):
    lowest, cutoff, highest = (bounds[0], bounds[1], bounds[2])
    half_width = (highest - cutoff) / 2.0
    centre = (highest + cutoff) / 2.0
    sigma_now = half_width / (lowest - centre)
    tau_value = 2.0 / sigma_now
    previous = start_block
    current = (operator_fn(start_block) - centre * start_block) * (sigma_now / half_width)
    for turn_index in range(DEGREE - 1):
        sigma_next = 1.0 / (tau_value - sigma_now)
        following = 2.0 * sigma_next / half_width * (operator_fn(current) - centre * current) - sigma_now * sigma_next * previous
        previous = current
        current = following
        sigma_now = sigma_next
    return current

def blocks_to_grid(blocks, counts, sides):
    trailing = blocks.shape[4:]
    shaped = blocks.reshape(tuple(counts) + tuple(sides) + trailing)
    axes_order = (0, 3, 1, 4, 2, 5) + tuple(range(6, 6 + len(trailing)))
    grid_shape = (counts[0] * sides[0], counts[1] * sides[1], counts[2] * sides[2]) + trailing
    return shaped.transpose(axes_order).reshape(grid_shape)

def grid_to_blocks(grid_field, counts, sides):
    trailing = grid_field.shape[3:]
    shaped = grid_field.reshape((counts[0], sides[0], counts[1], sides[1], counts[2], sides[2]) + trailing)
    axes_order = (0, 2, 4, 1, 3, 5) + tuple(range(6, 6 + len(trailing)))
    block_shape = (counts[0] * counts[1] * counts[2],) + tuple(sides) + trailing
    return shaped.transpose(axes_order).reshape(block_shape)

def contract(left, right):
    return lax.dot_general(left, right, (((0,), (0,)), ((), ())), precision=lax.Precision.HIGHEST, preferred_element_type=jnp.float32)

def reference(orbitals, potential, bounds, rotation):
    counts = (PX, PY, PZ)
    sides = (BX, BY, BZ)
    grid_orbitals = blocks_to_grid(orbitals, counts, sides)
    potential_grid = blocks_to_grid(potential, counts, sides)
    group_size = BANDS // N_BAND
    normed_list = []
    image_list = []
    for group_index in range(N_BAND):
        start_block = grid_orbitals[..., group_index * group_size:(group_index + 1) * group_size]
        operator_fn = lambda values: hamiltonian(values, potential_grid)
        filtered = chebyshev(start_block, operator_fn, bounds)
        band_norms = jnp.sqrt(lax.optimization_barrier(jnp.sum(filtered * filtered, axis=(0, 1, 2))))
        normed = filtered / band_norms
        normed_list.append(normed)
        image_list.append(hamiltonian(normed, potential_grid))
    normed_all = jnp.concatenate(normed_list, axis=3).reshape(-1, BANDS)
    image_all = jnp.concatenate(image_list, axis=3).reshape(-1, BANDS)
    margin = contract(normed_all, normed_all)
    projected = contract(normed_all, image_all)
    rotated = jnp.dot(normed_all, rotation, precision=lax.Precision.HIGHEST, preferred_element_type=jnp.float32)
    rotated = grid_to_blocks(rotated.reshape(NX, NY, NZ, BANDS), counts, sides)
    return (rotated, margin, projected)
```

```python
import itertools
from functools import partial

import jax
import jax.numpy as jnp
from jax import lax
from jax.experimental import pallas as pl
from jax.experimental.pallas import tpu as pltpu
from jax.sharding import PartitionSpec as P

STENCIL = (
    -5369.0 / 1800.0,
    12.0 / 7.0,
    -15.0 / 56.0,
    10.0 / 189.0,
    -1.0 / 112.0,
    2.0 / 1925.0,
    -1.0 / 16632.0,
)
REACH = 6
KINETIC = -0.5 / 0.36
BX, BY, BZ = 8, 12, 16
CELLS = BX * BY * BZ
HALF = CELLS // 2
PX, PY, PZ = 4, 4, 8
BLOCKS = PX * PY * PZ
LANES = 128

ORDER = [(ix * PY + iy) * PZ + iz for iz in range(PZ) for ix in range(PX) for iy in range(PY)]
STEP_X, STEP_Y, STEP_Z = PY, 1, PX * PY


def flat(band, dom):
    return band * BLOCKS + dom


def chip(y, x, z):
    return (y * 4 + x) * 4 + z


CORE_GROUPS = [[flat(2 * h + c, d) for d in ORDER for h in range(2)] for c in range(2)]
X_GROUPS = [
    [flat(b, chip(y, x, z)) for x in range(4)]
    for b in range(4)
    for y in range(8)
    for z in range(4)
]
PLANE_GROUPS = [
    [flat(2 * h + c, chip(y, x, z)) for y in range(8) for z in range(4) for h in range(2)]
    for c in range(2)
    for x in range(4)
]
CORE_SWAP = [(0, 1), (1, 0), (2, 3), (3, 2)]
Z_SWAP = [(0, 2), (2, 0), (1, 3), (3, 1)]


def exchange(x, groups):
    return lax.all_to_all(x, ("band", "dom"), 0, 0, tiled=True, axis_index_groups=groups)


OX, OY, OZ = REACH, REACH, 8
EXT = (BX + 2 * REACH, BY + 2 * REACH, BZ + 16, LANES)


def filter_kernel(coef_ref, x_ref, v_own_ref, v_other_ref, out_ref, ea, eb, pot, img):
    lane = lax.broadcasted_iota(jnp.int32, (1, LANES), 1)
    iz, ix, iy = lane // STEP_Z, lane // STEP_X % PX, lane % PY

    def spread(ext):
        own_y, own_z = slice(OY, OY + BY), slice(OZ, OZ + BZ)

        def below(v, step, keep):
            return jnp.where(keep, pltpu.roll(v, step, v.ndim - 1), 0.0)

        def above(v, step, keep):
            return jnp.where(keep, pltpu.roll(v, LANES - step, v.ndim - 1), 0.0)

        def inner(i, carry):
            at = i + OX
            ext[at, own_y, 0:8] = below(ext[at, own_y, OZ + 8 : OZ + 16], STEP_Z, iz > 0)
            ext[at, own_y, OZ + BZ : OZ + BZ + 8] = above(ext[at, own_y, OZ : OZ + 8], STEP_Z, iz < PZ - 1)
            ext[at, 0:OY, own_z] = below(ext[at, BY : BY + OY, own_z], STEP_Y, iy > 0)
            ext[at, OY + BY :, own_z] = above(ext[at, OY : 2 * OY, own_z], STEP_Y, iy < PY - 1)
            return carry

        def outer(i, carry):
            ext[i, own_y, own_z] = below(ext[i + BX, own_y, own_z], STEP_X, ix > 0)
            ext[i + OX + BX, own_y, own_z] = above(ext[i + OX, own_y, own_z], STEP_X, ix < PX - 1)
            return carry

        lax.fori_loop(0, BX, inner, 0)
        lax.fori_loop(0, REACH, outer, 0)

    def part(ext, i, y0, ys):
        return ext[i + OX, OY + y0 : OY + y0 + ys, OZ : OZ + BZ]

    def image(ext, i, y0, ys, scale, shift):
        at, y, z = i + OX, OY + y0, OZ
        centre = ext[at, y : y + ys, z : z + BZ]
        total = (3.0 * STENCIL[0]) * centre
        for k in range(1, REACH + 1):
            pair_x = ext[at - k, y : y + ys, z : z + BZ] + ext[at + k, y : y + ys, z : z + BZ]
            pair_y = ext[at, y - k : y - k + ys, z : z + BZ] + ext[at, y + k : y + k + ys, z : z + BZ]
            pair_z = ext[at, y : y + ys, z - k : z - k + BZ] + ext[at, y : y + ys, z + k : z + k + BZ]
            total = total + STENCIL[k] * ((pair_x + pair_y) + pair_z)
        local = pot[i, y0 : y0 + ys] - shift
        return (scale * KINETIC) * total + scale * (local * centre)

    second = coef_ref[7]
    for q in range(CELLS // LANES):
        cells = slice(q * LANES, (q + 1) * LANES)
        tile = jnp.transpose(x_ref[:, cells]).reshape(LANES // BZ, BZ, LANES)
        at = q % (HALF // LANES) * LANES
        own, other = v_own_ref[:, at : at + LANES], v_other_ref[:, at : at + LANES]
        swap = second > 0.5 if q < HALF // LANES else second < 0.5
        vtile = jnp.transpose(jnp.where(swap, other, own)).reshape(LANES // BZ, BZ, LANES)
        for r in range(LANES // BZ):
            row = q * (LANES // BZ) + r
            ea[OX + row // BY, OY + row % BY, OZ : OZ + BZ] = tile[r]
            pot[row // BY, row % BY] = vtile[r]

    ys = BY // 2

    def first(i, carry):
        for y0 in range(0, BY, ys):
            eb[i + OX, OY + y0 : OY + y0 + ys, OZ : OZ + BZ] = image(ea, i, y0, ys, coef_ref[0], coef_ref[1])
        return carry

    def later(src, dst, scale, back):
        def body(i, squares):
            for y0 in range(0, BY, ys):
                new = image(src, i, y0, ys, scale, coef_ref[1]) - back * part(dst, i, y0, ys)
                dst[i + OX, OY + y0 : OY + y0 + ys, OZ : OZ + BZ] = new
                squares = squares + jnp.sum(new * new, axis=0)
            return squares

        return body

    def last(i, carry):
        for y0 in range(0, BY, ys):
            img[i, y0 : y0 + ys] = image(eb, i, y0, ys, 1.0, 0.0)
        return carry

    zero = jnp.zeros((BZ, LANES), jnp.float32)
    spread(ea)
    lax.fori_loop(0, BX, first, 0)
    spread(eb)
    lax.fori_loop(0, BX, later(eb, ea, coef_ref[2], coef_ref[3]), zero)
    spread(ea)
    squares = lax.fori_loop(0, BX, later(ea, eb, coef_ref[4], coef_ref[5]), zero)
    spread(eb)
    lax.fori_loop(0, BX, last, 0)
    norm = jnp.sqrt(jnp.sum(squares, keepdims=True))
    for q in range(CELLS // LANES):
        rows = [q * (LANES // BZ) + r for r in range(LANES // BZ)]
        at = q // (HALF // LANES) * CELLS + q % (HALF // LANES) * LANES
        field = jnp.concatenate([eb[OX + r // BY, OY + r % BY, OZ : OZ + BZ] for r in rows], 0)
        out_ref[:, at : at + LANES] = jnp.transpose(field / norm)
        field = jnp.concatenate([img[r // BY, r % BY] for r in rows], 0)
        out_ref[:, at + HALF : at + HALF + LANES] = jnp.transpose(field / norm)


def filtered_fields(coef, x, v_own, v_other):
    vmem = pl.BlockSpec(memory_space=pltpu.VMEM)
    return pl.pallas_call(
        filter_kernel,
        out_shape=jax.ShapeDtypeStruct((BLOCKS, 2 * CELLS), jnp.float32),
        in_specs=[pl.BlockSpec(memory_space=pltpu.SMEM), vmem, vmem, vmem],
        out_specs=vmem,
        scratch_shapes=[
            pltpu.VMEM(EXT, jnp.float32),
            pltpu.VMEM(EXT, jnp.float32),
            pltpu.VMEM((BX, BY, BZ, LANES), jnp.float32),
            pltpu.VMEM((BX, BY, BZ, LANES), jnp.float32),
        ],
        compiler_params=pltpu.CompilerParams(vmem_limit_bytes=40 * 1024 * 1024),
    )(coef, x, v_own, v_other)


def filter_coefficients(bounds, second):
    lowest, cutoff, highest = bounds[0], bounds[1], bounds[2]
    half_width = (highest - cutoff) / 2.0
    centre = (highest + cutoff) / 2.0
    s1 = half_width / (lowest - centre)
    tau = 2.0 / s1
    s2 = 1.0 / (tau - s1)
    s3 = 1.0 / (tau - s2)
    return jnp.stack(
        [
            s1 / half_width,
            centre,
            2.0 * s2 / half_width,
            s1 * s2,
            2.0 * s3 / half_width,
            s2 * s3,
            jnp.float32(0.0),
            second,
        ]
    )


def contract(left, right, dims):
    return lax.dot_general(
        left,
        right,
        (dims, ((), ())),
        precision=lax.Precision.HIGH,
        preferred_element_type=jnp.float32,
    )


def local(orbitals, potential, bounds, rotation):
    width = rotation.shape[1]
    band = lax.axis_index("band")
    z_hi, core = band // 2, band % 2
    coef = filter_coefficients(bounds, core.astype(jnp.float32))
    rotation_far = lax.ppermute(rotation, "band", Z_SWAP)

    fields = orbitals.reshape(CELLS, width).T
    half = lax.dynamic_slice_in_dim(potential.reshape(CELLS), core * HALF, HALF)
    sent = jnp.concatenate([fields, jnp.broadcast_to(half[None], (BLOCKS, HALF))], axis=1)
    got = lax.all_to_all(sent, "dom", 0, 0, tiled=True, axis_index_groups=[ORDER])
    v_own = got[:, CELLS:]
    v_other = lax.ppermute(v_own, "band", CORE_SWAP)
    images = filtered_fields(coef, got[:, :CELLS], v_own, v_other)

    got = exchange(images.reshape(2 * BLOCKS, CELLS), CORE_GROUPS)
    got = got.reshape(BLOCKS, 2, 2, HALF).transpose(1, 2, 0, 3)
    phi = got[:, 0].reshape(2 * BLOCKS, HALF)
    phi_other = lax.ppermute(phi, "band", CORE_SWAP)
    phi_all = jnp.concatenate([phi, phi_other], axis=0)
    columns = got.transpose(1, 0, 2, 3).reshape(4 * BLOCKS, HALF)
    gram = contract(phi_all, columns, ((1,), (1,)))

    def by_core(weights):
        weights = weights.reshape(2, 2, BLOCKS, width)
        swapped = jnp.where(core == 0, weights, weights[:, ::-1])
        return swapped.transpose(1, 0, 2, 3).reshape(4 * BLOCKS, width)

    rotated_far = contract(phi_all, by_core(rotation_far), ((0,), (0,)))
    rotated_far = lax.ppermute(rotated_far, "band", Z_SWAP)
    rotated_near = contract(phi_all, by_core(rotation), ((0,), (0,)))

    terms = exchange(gram.reshape(4, BLOCKS, 4 * BLOCKS), X_GROUPS)
    terms = jnp.sum(terms, axis=0)
    terms = terms.reshape(32, 4, 2, 2, BLOCKS).transpose(0, 3, 1, 2, 4).reshape(64, 8 * BLOCKS)
    terms = jnp.sum(exchange(terms, PLANE_GROUPS), axis=0)
    whole = lax.all_to_all(
        jnp.broadcast_to(terms[None], (BLOCKS, 8 * BLOCKS)), "dom", 0, 0, tiled=True
    )
    whole = whole.reshape(8, 2, 2, 4, 4, 2, BLOCKS).transpose(5, 2, 1, 0, 3, 4, 6)
    whole = whole.reshape(2, 2, 2, BLOCKS, BLOCKS)
    whole = jnp.where(core == 0, whole, whole[:, :, ::-1])
    whole = whole.reshape(2, 4 * BLOCKS, BLOCKS)
    lower = jnp.where(z_hi == 0, rotated_near, rotated_far)
    upper = jnp.where(z_hi == 0, rotated_far, rotated_near)
    rotated = jnp.concatenate([lower, upper], axis=0).reshape(1, BX, BY, BZ, width)
    return (rotated, whole[0], whole[1])


def solution(mesh):
    in_specs = (
        P("dom", None, None, None, "band"),
        P("dom", None, None, None),
        P(),
        P(None, "band"),
    )
    out_specs = (P("dom", None, None, None, "band"), P(None, "band"), P(None, "band"))
    return jax.shard_map(local, mesh=mesh, in_specs=in_specs, out_specs=out_specs, check_vma=False)
```

```python
import itertools
from functools import partial

import jax
import jax.numpy as jnp
from jax import lax
from jax.experimental import pallas as pl
from jax.experimental.pallas import tpu as pltpu
from jax.sharding import PartitionSpec as P

STENCIL = (
    -5369.0 / 1800.0,
    12.0 / 7.0,
    -15.0 / 56.0,
    10.0 / 189.0,
    -1.0 / 112.0,
    2.0 / 1925.0,
    -1.0 / 16632.0,
)
REACH = 6
KINETIC = -0.5 / 0.36
BX, BY, BZ = 8, 12, 16
CELLS = BX * BY * BZ
HALF = CELLS // 2
PX, PY, PZ = 4, 4, 8
BLOCKS = PX * PY * PZ
LANES = 128
TILES = CELLS // LANES
HALF_TILES = HALF // LANES
SENT = TILES + HALF_TILES

ORDER = [(ix * PY + iy) * PZ + iz for iz in range(PZ) for ix in range(PX) for iy in range(PY)]
STEP_X, STEP_Y, STEP_Z = PY, 1, PX * PY


def flat(band, dom):
    return band * BLOCKS + dom


def chip(y, x, z):
    return (y * 4 + x) * 4 + z


CORE_GROUPS = [[flat(2 * h + c, d) for d in ORDER for h in range(2)] for c in range(2)]
X_GROUPS = [
    [flat(b, chip(y, x, z)) for x in range(4)]
    for b in range(4)
    for y in range(8)
    for z in range(4)
]
PLANE_GROUPS = [
    [flat(2 * h + c, chip(y, x, z)) for y in range(8) for z in range(4) for h in range(2)]
    for c in range(2)
    for x in range(4)
]
CORE_SWAP = [(0, 1), (1, 0), (2, 3), (3, 2)]
Z_SWAP = [(0, 2), (2, 0), (1, 3), (3, 1)]


def exchange(x, groups):
    return lax.all_to_all(x, ("band", "dom"), 0, 0, tiled=True, axis_index_groups=groups)


OX, OY, OZ = REACH, REACH, 8
EXT = (BX + 2 * REACH, BY + 2 * REACH, BZ + 16, LANES)


def pack_kernel(core_ref, orbitals_ref, potential_ref, out_ref, wide):
    for t in range(TILES):
        tile = orbitals_ref[t * LANES : (t + 1) * LANES]
        out_ref[pl.ds(t, BLOCKS, stride=SENT), :] = jnp.transpose(tile)
    wide[...] = jnp.concatenate([potential_ref[i] for i in range(BX)], axis=1)
    for s in range(HALF_TILES):
        row = wide[pl.ds(core_ref[0] * HALF_TILES + s, 1), :]
        out_ref[pl.ds(TILES + s, BLOCKS, stride=SENT), :] = jnp.broadcast_to(row, (BLOCKS, LANES))


def packed(core, orbitals, potential):
    vmem = pl.BlockSpec(memory_space=pltpu.VMEM)
    return pl.pallas_call(
        pack_kernel,
        out_shape=jax.ShapeDtypeStruct((BLOCKS * SENT, LANES), jnp.float32),
        in_specs=[pl.BlockSpec(memory_space=pltpu.SMEM), vmem, vmem],
        out_specs=vmem,
        scratch_shapes=[pltpu.VMEM((BY, BX * BZ), jnp.float32)],
        compiler_params=pltpu.CompilerParams(vmem_limit_bytes=16 * 1024 * 1024),
    )(core, orbitals, potential)


def split_kernel(got_ref, phi_ref, both_ref):
    for m in range(2):
        for h in range(2):
            for t in range(HALF_TILES):
                tile = got_ref[pl.ds(h * TILES + m * HALF_TILES + t, BLOCKS, stride=2 * TILES), :]
                cells = slice(t * LANES, (t + 1) * LANES)
                at = (2 * m + h) * BLOCKS
                both_ref[at : at + BLOCKS, cells] = tile
                if m == 0:
                    phi_ref[at : at + BLOCKS, cells] = tile


def split_fields(got):
    vmem = pl.BlockSpec(memory_space=pltpu.VMEM)
    return pl.pallas_call(
        split_kernel,
        out_shape=(
            jax.ShapeDtypeStruct((2 * BLOCKS, HALF), jnp.float32),
            jax.ShapeDtypeStruct((4 * BLOCKS, HALF), jnp.float32),
        ),
        in_specs=[vmem],
        out_specs=(vmem, vmem),
        compiler_params=pltpu.CompilerParams(vmem_limit_bytes=16 * 1024 * 1024),
    )(got)


def filter_kernel(coef_ref, got_ref, v_other_ref, out_ref, ea, eb, pot, img):
    lane = lax.broadcasted_iota(jnp.int32, (1, LANES), 1)
    iz, ix, iy = lane // STEP_Z, lane // STEP_X % PX, lane % PY

    def spread(ext):
        own_y, own_z = slice(OY, OY + BY), slice(OZ, OZ + BZ)

        def below(v, step, keep):
            return jnp.where(keep, pltpu.roll(v, step, v.ndim - 1), 0.0)

        def above(v, step, keep):
            return jnp.where(keep, pltpu.roll(v, LANES - step, v.ndim - 1), 0.0)

        def inner(i, carry):
            at = i + OX
            ext[at, own_y, 0:8] = below(ext[at, own_y, OZ + 8 : OZ + 16], STEP_Z, iz > 0)
            ext[at, own_y, OZ + BZ : OZ + BZ + 8] = above(ext[at, own_y, OZ : OZ + 8], STEP_Z, iz < PZ - 1)
            ext[at, 0:OY, own_z] = below(ext[at, BY : BY + OY, own_z], STEP_Y, iy > 0)
            ext[at, OY + BY :, own_z] = above(ext[at, OY : 2 * OY, own_z], STEP_Y, iy < PY - 1)
            return carry

        def outer(i, carry):
            ext[i, own_y, own_z] = below(ext[i + BX, own_y, own_z], STEP_X, ix > 0)
            ext[i + OX + BX, own_y, own_z] = above(ext[i + OX, own_y, own_z], STEP_X, ix < PX - 1)
            return carry

        lax.fori_loop(0, BX, inner, 0)
        lax.fori_loop(0, REACH, outer, 0)

    def part(ext, i, y0, ys):
        return ext[i + OX, OY + y0 : OY + y0 + ys, OZ : OZ + BZ]

    def image(ext, i, y0, ys, scale, shift):
        at, y, z = i + OX, OY + y0, OZ
        centre = ext[at, y : y + ys, z : z + BZ]
        total = (3.0 * STENCIL[0]) * centre
        for k in range(1, REACH + 1):
            pair_x = ext[at - k, y : y + ys, z : z + BZ] + ext[at + k, y : y + ys, z : z + BZ]
            pair_y = ext[at, y - k : y - k + ys, z : z + BZ] + ext[at, y + k : y + k + ys, z : z + BZ]
            pair_z = ext[at, y : y + ys, z - k : z - k + BZ] + ext[at, y : y + ys, z + k : z + k + BZ]
            total = total + STENCIL[k] * ((pair_x + pair_y) + pair_z)
        local = pot[i, y0 : y0 + ys] - shift
        return (scale * KINETIC) * total + scale * (local * centre)

    second = coef_ref[7]
    for q in range(TILES):
        tile = jnp.transpose(got_ref[pl.ds(q, BLOCKS, stride=SENT), :]).reshape(LANES // BZ, BZ, LANES)
        for r in range(LANES // BZ):
            row = q * (LANES // BZ) + r
            ea[OX + row // BY, OY + row % BY, OZ : OZ + BZ] = tile[r]
    for y in range(BY):
        s = y % HALF_TILES
        own = got_ref[pl.ds(TILES + s, BLOCKS, stride=SENT), :]
        other = v_other_ref[pl.ds(s, BLOCKS, stride=HALF_TILES), :]
        swap = second > 0.5 if y < HALF_TILES else second < 0.5
        pot[:, y] = jnp.transpose(jnp.where(swap, other, own)).reshape(BX, BZ, LANES)

    ys = BY // 2

    def first(i, carry):
        for y0 in range(0, BY, ys):
            eb[i + OX, OY + y0 : OY + y0 + ys, OZ : OZ + BZ] = image(ea, i, y0, ys, coef_ref[0], coef_ref[1])
        return carry

    def later(src, dst, scale, back):
        def body(i, squares):
            for y0 in range(0, BY, ys):
                new = image(src, i, y0, ys, scale, coef_ref[1]) - back * part(dst, i, y0, ys)
                dst[i + OX, OY + y0 : OY + y0 + ys, OZ : OZ + BZ] = new
                squares = squares + jnp.sum(new * new, axis=0)
            return squares

        return body

    def last(i, carry):
        for y0 in range(0, BY, ys):
            img[i, y0 : y0 + ys] = image(eb, i, y0, ys, 1.0, 0.0)
        return carry

    zero = jnp.zeros((BZ, LANES), jnp.float32)
    spread(ea)
    lax.fori_loop(0, BX, first, 0)
    spread(eb)
    lax.fori_loop(0, BX, later(eb, ea, coef_ref[2], coef_ref[3]), zero)
    spread(ea)
    squares = lax.fori_loop(0, BX, later(ea, eb, coef_ref[4], coef_ref[5]), zero)
    spread(eb)
    lax.fori_loop(0, BX, last, 0)
    norm = jnp.sqrt(jnp.sum(squares, keepdims=True))
    for q in range(TILES):
        rows = [q * (LANES // BZ) + r for r in range(LANES // BZ)]
        at = q // HALF_TILES * TILES + q % HALF_TILES
        field = jnp.concatenate([eb[OX + r // BY, OY + r % BY, OZ : OZ + BZ] for r in rows], 0)
        out_ref[pl.ds(at, BLOCKS, stride=2 * TILES), :] = jnp.transpose(field / norm)
        field = jnp.concatenate([img[r // BY, r % BY] for r in rows], 0)
        out_ref[pl.ds(at + HALF_TILES, BLOCKS, stride=2 * TILES), :] = jnp.transpose(field / norm)


def filtered_fields(coef, got, v_other):
    vmem = pl.BlockSpec(memory_space=pltpu.VMEM)
    return pl.pallas_call(
        filter_kernel,
        out_shape=jax.ShapeDtypeStruct((BLOCKS * 2 * TILES, LANES), jnp.float32),
        in_specs=[pl.BlockSpec(memory_space=pltpu.SMEM), vmem, vmem],
        out_specs=vmem,
        scratch_shapes=[
            pltpu.VMEM(EXT, jnp.float32),
            pltpu.VMEM(EXT, jnp.float32),
            pltpu.VMEM((BX, BY, BZ, LANES), jnp.float32),
            pltpu.VMEM((BX, BY, BZ, LANES), jnp.float32),
        ],
        compiler_params=pltpu.CompilerParams(vmem_limit_bytes=40 * 1024 * 1024),
    )(coef, got, v_other)


def filter_coefficients(bounds, second):
    lowest, cutoff, highest = bounds[0], bounds[1], bounds[2]
    half_width = (highest - cutoff) / 2.0
    centre = (highest + cutoff) / 2.0
    s1 = half_width / (lowest - centre)
    tau = 2.0 / s1
    s2 = 1.0 / (tau - s1)
    s3 = 1.0 / (tau - s2)
    return jnp.stack(
        [
            s1 / half_width,
            centre,
            2.0 * s2 / half_width,
            s1 * s2,
            2.0 * s3 / half_width,
            s2 * s3,
            jnp.float32(0.0),
            second,
        ]
    )


def contract(left, right, dims):
    return lax.dot_general(
        left,
        right,
        (dims, ((), ())),
        precision=lax.Precision.HIGH,
        preferred_element_type=jnp.float32,
    )


def local(orbitals, potential, bounds, rotation):
    width = rotation.shape[1]
    band = lax.axis_index("band")
    z_hi, core = band // 2, band % 2
    coef = filter_coefficients(bounds, core.astype(jnp.float32))
    rotation_far = lax.ppermute(rotation, "band", Z_SWAP)

    sent = packed(core.reshape(1), orbitals.reshape(CELLS, width), potential[0])
    got = lax.all_to_all(
        sent.reshape(BLOCKS, 1, SENT * LANES), "dom", 0, 0, tiled=True, axis_index_groups=[ORDER]
    )
    got, rotation_far = lax.optimization_barrier((got, rotation_far))
    v_other = lax.ppermute(got[:, :, CELLS:], "band", CORE_SWAP)
    images = filtered_fields(
        coef, got.reshape(BLOCKS * SENT, LANES), v_other.reshape(BLOCKS * HALF_TILES, LANES)
    )

    got = exchange(images.reshape(2 * BLOCKS, 1, CELLS), CORE_GROUPS)
    phi, both = split_fields(got.reshape(2 * BLOCKS * TILES, LANES))
    phi_other = lax.ppermute(phi, "band", CORE_SWAP)
    gram = jnp.concatenate(
        [contract(phi, both, ((1,), (1,))), contract(phi_other, both, ((1,), (1,)))], axis=0
    )

    def by_core(weights):
        weights = weights.reshape(2, 2, BLOCKS, width)
        swapped = jnp.where(core == 0, weights, weights[:, ::-1])
        return swapped.transpose(1, 0, 2, 3).reshape(4 * BLOCKS, width)

    def rotate(weights):
        weights = by_core(weights)
        return contract(phi, weights[: 2 * BLOCKS], ((0,), (0,))) + contract(
            phi_other, weights[2 * BLOCKS :], ((0,), (0,))
        )

    rotated_far = rotate(rotation_far)
    gram, rotated_far = lax.optimization_barrier((gram, rotated_far))
    rotated_far = lax.ppermute(rotated_far, "band", Z_SWAP)
    rotated_near = rotate(rotation)

    terms = exchange(gram.reshape(4, BLOCKS, 4 * BLOCKS), X_GROUPS)
    terms = jnp.sum(terms, axis=0)
    terms = terms.reshape(32, 4, 2, 2, BLOCKS).transpose(0, 3, 1, 2, 4).reshape(64, 8 * BLOCKS)
    terms = exchange(terms.reshape(64, 1, 8 * BLOCKS), PLANE_GROUPS)
    terms, rotated_far = lax.optimization_barrier((terms, rotated_far))
    terms = jnp.sum(terms, axis=0)
    whole = lax.all_to_all(
        jnp.broadcast_to(terms[None], (BLOCKS, 1, 8 * BLOCKS)), "dom", 0, 0, tiled=True
    )
    whole = whole.reshape(8, 2, 2, 4, 4, 2, BLOCKS).transpose(5, 2, 1, 0, 3, 4, 6)
    whole = whole.reshape(2, 2, 2, BLOCKS, BLOCKS)
    whole = jnp.where(core == 0, whole, whole[:, :, ::-1])
    whole = whole.reshape(2, 4 * BLOCKS, BLOCKS)
    lower = jnp.where(z_hi == 0, rotated_near, rotated_far)
    upper = jnp.where(z_hi == 0, rotated_far, rotated_near)
    rotated = jnp.concatenate([lower, upper], axis=0).reshape(1, BX, BY, BZ, width)
    return (rotated, whole[0], whole[1])


def solution(mesh):
    in_specs = (
        P("dom", None, None, None, "band"),
        P("dom", None, None, None),
        P(),
        P(None, "band"),
    )
    out_specs = (P("dom", None, None, None, "band"), P(None, "band"), P(None, "band"))
    return jax.shard_map(local, mesh=mesh, in_specs=in_specs, out_specs=out_specs, check_vma=False)
```

```python
import jax
import jax.numpy as jnp
from jax import lax
from jax.experimental import pallas as pl
from jax.experimental.pallas import tpu as pltpu
from jax.sharding import PartitionSpec as P

STENCIL = (
    -5369.0 / 1800.0,
    12.0 / 7.0,
    -15.0 / 56.0,
    10.0 / 189.0,
    -1.0 / 112.0,
    2.0 / 1925.0,
    -1.0 / 16632.0,
)
REACH = 6
KINETIC = -0.5 / 0.36
BX, BY, BZ = 8, 12, 16
CELLS = BX * BY * BZ
HALF = CELLS // 2
PX, PY, PZ = 4, 4, 8
BLOCKS = PX * PY * PZ
LANES = 128
TILES = CELLS // LANES
HALF_TILES = HALF // LANES
SENT = TILES + HALF_TILES

ORDER = [(ix * PY + iy) * PZ + iz for iz in range(PZ) for iy in range(PY) for ix in range(PX)]
STEP_X, STEP_Y, STEP_Z = 1, PX, PX * PY


def flat(band, dom):
    return band * BLOCKS + dom


def chip(y, x, z):
    return (y * 4 + x) * 4 + z


CORE_GROUPS = [[flat(2 * h + c, d) for d in ORDER for h in range(2)] for c in range(2)]
X_GROUPS = [
    [flat(b, chip(y, x, z)) for x in range(4)]
    for b in range(4)
    for y in range(8)
    for z in range(4)
]
PLANE_GROUPS = [
    [flat(2 * h + c, chip(y, x, z)) for y in range(8) for z in range(4) for h in range(2)]
    for c in range(2)
    for x in range(4)
]
CORE_SWAP = [(0, 1), (1, 0), (2, 3), (3, 2)]
Z_SWAP = [(0, 2), (2, 0), (1, 3), (3, 1)]


def exchange(x, groups):
    return lax.all_to_all(x, ("band", "dom"), 0, 0, tiled=True, axis_index_groups=groups)


OX, OY, OZ = REACH, REACH, 8
EXT = (BX + 2 * REACH, BY + 2 * REACH, BZ + 16, LANES)


def pack_kernel(core_ref, orbitals_ref, potential_ref, out_ref, wide):
    for t in range(TILES):
        tile = orbitals_ref[t * LANES : (t + 1) * LANES]
        out_ref[pl.ds(t, BLOCKS, stride=SENT), :] = jnp.transpose(tile)
    wide[...] = jnp.concatenate([potential_ref[i] for i in range(BX)], axis=1)
    for s in range(HALF_TILES):
        row = wide[pl.ds(core_ref[0] * HALF_TILES + s, 1), :]
        out_ref[pl.ds(TILES + s, BLOCKS, stride=SENT), :] = jnp.broadcast_to(row, (BLOCKS, LANES))


def packed(core, orbitals, potential):
    vmem = pl.BlockSpec(memory_space=pltpu.VMEM)
    return pl.pallas_call(
        pack_kernel,
        out_shape=jax.ShapeDtypeStruct((BLOCKS * SENT, LANES), jnp.float32),
        in_specs=[pl.BlockSpec(memory_space=pltpu.SMEM), vmem, vmem],
        out_specs=vmem,
        scratch_shapes=[pltpu.VMEM((BY, BX * BZ), jnp.float32)],
        compiler_params=pltpu.CompilerParams(vmem_limit_bytes=16 * 1024 * 1024),
    )(core, orbitals, potential)


def split_kernel(got_ref, phi_ref, both_ref):
    for m in range(2):
        for h in range(2):
            for t in range(HALF_TILES):
                tile = got_ref[pl.ds(h * TILES + m * HALF_TILES + t, BLOCKS, stride=2 * TILES), :]
                cells = slice(t * LANES, (t + 1) * LANES)
                at = (2 * m + h) * BLOCKS
                both_ref[at : at + BLOCKS, cells] = tile
                if m == 0:
                    phi_ref[at : at + BLOCKS, cells] = tile


def split_fields(got):
    vmem = pl.BlockSpec(memory_space=pltpu.VMEM)
    return pl.pallas_call(
        split_kernel,
        out_shape=(
            jax.ShapeDtypeStruct((2 * BLOCKS, HALF), jnp.float32),
            jax.ShapeDtypeStruct((4 * BLOCKS, HALF), jnp.float32),
        ),
        in_specs=[vmem],
        out_specs=(vmem, vmem),
        compiler_params=pltpu.CompilerParams(vmem_limit_bytes=16 * 1024 * 1024),
    )(got)


def filter_kernel(coef_ref, got_ref, v_other_ref, out_ref, ea, eb, pot, img):
    lane = lax.broadcasted_iota(jnp.int32, (1, LANES), 1)
    iz, iy, ix = lane // STEP_Z, lane // STEP_Y % PY, lane // STEP_X % PX

    def spread(ext):
        own_y, own_z = slice(OY, OY + BY), slice(OZ, OZ + BZ)

        def below(v, step, keep):
            return jnp.where(keep, pltpu.roll(v, step, v.ndim - 1), 0.0)

        def above(v, step, keep):
            return jnp.where(keep, pltpu.roll(v, LANES - step, v.ndim - 1), 0.0)

        def inner(i, carry):
            at = i + OX
            ext[at, own_y, 0:8] = below(ext[at, own_y, OZ + 8 : OZ + 16], STEP_Z, iz > 0)
            ext[at, own_y, OZ + BZ : OZ + BZ + 8] = above(ext[at, own_y, OZ : OZ + 8], STEP_Z, iz < PZ - 1)
            ext[at, 0:OY, own_z] = below(ext[at, BY : BY + OY, own_z], STEP_Y, iy > 0)
            ext[at, OY + BY :, own_z] = above(ext[at, OY : 2 * OY, own_z], STEP_Y, iy < PY - 1)
            return carry

        def outer(i, carry):
            ext[i, own_y, own_z] = below(ext[i + BX, own_y, own_z], STEP_X, ix > 0)
            ext[i + OX + BX, own_y, own_z] = above(ext[i + OX, own_y, own_z], STEP_X, ix < PX - 1)
            return carry

        lax.fori_loop(0, BX, inner, 0)
        lax.fori_loop(0, REACH, outer, 0)

    def part(ext, i, y0, ys):
        return ext[i + OX, OY + y0 : OY + y0 + ys, OZ : OZ + BZ]

    def image(ext, i, y0, ys, scale, shift):
        at, y, z = i + OX, OY + y0, OZ
        centre = ext[at, y : y + ys, z : z + BZ]
        total = (3.0 * STENCIL[0]) * centre
        for k in range(1, REACH + 1):
            pair_x = ext[at - k, y : y + ys, z : z + BZ] + ext[at + k, y : y + ys, z : z + BZ]
            pair_y = ext[at, y - k : y - k + ys, z : z + BZ] + ext[at, y + k : y + k + ys, z : z + BZ]
            pair_z = ext[at, y : y + ys, z - k : z - k + BZ] + ext[at, y : y + ys, z + k : z + k + BZ]
            total = total + STENCIL[k] * ((pair_x + pair_y) + pair_z)
        local = pot[i, y0 : y0 + ys] - shift
        return (scale * KINETIC) * total + scale * (local * centre)

    second = coef_ref[7]
    for q in range(TILES):
        tile = jnp.transpose(got_ref[pl.ds(q, BLOCKS, stride=SENT), :]).reshape(LANES // BZ, BZ, LANES)
        for r in range(LANES // BZ):
            row = q * (LANES // BZ) + r
            ea[OX + row // BY, OY + row % BY, OZ : OZ + BZ] = tile[r]
    for y in range(BY):
        s = y % HALF_TILES
        own = got_ref[pl.ds(TILES + s, BLOCKS, stride=SENT), :]
        other = v_other_ref[pl.ds(s, BLOCKS, stride=HALF_TILES), :]
        swap = second > 0.5 if y < HALF_TILES else second < 0.5
        pot[:, y] = jnp.transpose(jnp.where(swap, other, own)).reshape(BX, BZ, LANES)

    ys = BY // 2

    def first(i, carry):
        for y0 in range(0, BY, ys):
            eb[i + OX, OY + y0 : OY + y0 + ys, OZ : OZ + BZ] = image(ea, i, y0, ys, coef_ref[0], coef_ref[1])
        return carry

    def later(src, dst, scale, back):
        def body(i, squares):
            for y0 in range(0, BY, ys):
                new = image(src, i, y0, ys, scale, coef_ref[1]) - back * part(dst, i, y0, ys)
                dst[i + OX, OY + y0 : OY + y0 + ys, OZ : OZ + BZ] = new
                squares = squares + jnp.sum(new * new, axis=0)
            return squares

        return body

    def last(i, carry):
        for y0 in range(0, BY, ys):
            img[i, y0 : y0 + ys] = image(eb, i, y0, ys, 1.0, 0.0)
        return carry

    zero = jnp.zeros((BZ, LANES), jnp.float32)
    spread(ea)
    lax.fori_loop(0, BX, first, 0)
    spread(eb)
    lax.fori_loop(0, BX, later(eb, ea, coef_ref[2], coef_ref[3]), zero)
    spread(ea)
    squares = lax.fori_loop(0, BX, later(ea, eb, coef_ref[4], coef_ref[5]), zero)
    spread(eb)
    lax.fori_loop(0, BX, last, 0)
    norm = jnp.sqrt(jnp.sum(squares, keepdims=True))
    for q in range(TILES):
        rows = [q * (LANES // BZ) + r for r in range(LANES // BZ)]
        at = q // HALF_TILES * TILES + q % HALF_TILES
        field = jnp.concatenate([eb[OX + r // BY, OY + r % BY, OZ : OZ + BZ] for r in rows], 0)
        out_ref[pl.ds(at, BLOCKS, stride=2 * TILES), :] = jnp.transpose(field / norm)
        field = jnp.concatenate([img[r // BY, r % BY] for r in rows], 0)
        out_ref[pl.ds(at + HALF_TILES, BLOCKS, stride=2 * TILES), :] = jnp.transpose(field / norm)


def filtered_fields(coef, got, v_other):
    vmem = pl.BlockSpec(memory_space=pltpu.VMEM)
    return pl.pallas_call(
        filter_kernel,
        out_shape=jax.ShapeDtypeStruct((BLOCKS * 2 * TILES, LANES), jnp.float32),
        in_specs=[pl.BlockSpec(memory_space=pltpu.SMEM), vmem, vmem],
        out_specs=vmem,
        scratch_shapes=[
            pltpu.VMEM(EXT, jnp.float32),
            pltpu.VMEM(EXT, jnp.float32),
            pltpu.VMEM((BX, BY, BZ, LANES), jnp.float32),
            pltpu.VMEM((BX, BY, BZ, LANES), jnp.float32),
        ],
        compiler_params=pltpu.CompilerParams(vmem_limit_bytes=40 * 1024 * 1024),
    )(coef, got, v_other)


def filter_coefficients(bounds, second):
    lowest, cutoff, highest = bounds[0], bounds[1], bounds[2]
    half_width = (highest - cutoff) / 2.0
    centre = (highest + cutoff) / 2.0
    s1 = half_width / (lowest - centre)
    tau = 2.0 / s1
    s2 = 1.0 / (tau - s1)
    s3 = 1.0 / (tau - s2)
    return jnp.stack(
        [
            s1 / half_width,
            centre,
            2.0 * s2 / half_width,
            s1 * s2,
            2.0 * s3 / half_width,
            s2 * s3,
            jnp.float32(0.0),
            second,
        ]
    )


def contract(left, right, dims):
    return lax.dot_general(
        left,
        right,
        (dims, ((), ())),
        precision=lax.Precision.HIGH,
        preferred_element_type=jnp.float32,
    )


def local(orbitals, potential, bounds, rotation):
    width = rotation.shape[1]
    band = lax.axis_index("band")
    z_hi, core = band // 2, band % 2
    coef = filter_coefficients(bounds, core.astype(jnp.float32))

    sent = packed(core.reshape(1), orbitals.reshape(CELLS, width), potential[0])
    got = lax.all_to_all(
        sent.reshape(BLOCKS, 1, SENT * LANES), "dom", 0, 0, tiled=True, axis_index_groups=[ORDER]
    )
    got, rotation_near = lax.optimization_barrier((got, rotation))
    rotation_far = lax.ppermute(rotation_near, "band", Z_SWAP)
    v_other = lax.ppermute(got[:, :, CELLS:], "band", CORE_SWAP)
    images = filtered_fields(
        coef, got.reshape(BLOCKS * SENT, LANES), v_other.reshape(BLOCKS * HALF_TILES, LANES)
    )

    images, rotation_far = lax.optimization_barrier((images, rotation_far))
    got = exchange(images.reshape(2 * BLOCKS, 1, CELLS), CORE_GROUPS)
    got, rotation_near, rotation_far = lax.optimization_barrier((got, rotation_near, rotation_far))
    phi, both = split_fields(got.reshape(2 * BLOCKS * TILES, LANES))
    phi_other = lax.ppermute(phi, "band", CORE_SWAP)
    gram = jnp.concatenate(
        [contract(phi, both, ((1,), (1,))), contract(phi_other, both, ((1,), (1,)))], axis=0
    )

    def by_core(weights):
        weights = weights.reshape(2, 2, BLOCKS, width)
        swapped = jnp.where(core == 0, weights, weights[:, ::-1])
        return swapped.transpose(1, 0, 2, 3).reshape(4 * BLOCKS, width)

    def rotate(weights):
        weights = by_core(weights)
        return contract(phi, weights[: 2 * BLOCKS], ((0,), (0,))) + contract(
            phi_other, weights[2 * BLOCKS :], ((0,), (0,))
        )

    rotated_far = rotate(rotation_far)
    gram, rotated_far = lax.optimization_barrier((gram, rotated_far))
    rotated_far = lax.ppermute(rotated_far, "band", Z_SWAP)
    rotated_near = rotate(rotation_near)

    terms = exchange(gram.reshape(4, BLOCKS, 4 * BLOCKS), X_GROUPS)
    terms, rotated_far = lax.optimization_barrier((terms, rotated_far))
    terms = jnp.sum(terms, axis=0)
    terms = terms.reshape(32, 4, 2, 2, BLOCKS).transpose(0, 3, 1, 2, 4).reshape(64, 8 * BLOCKS)
    terms = exchange(terms.reshape(64, 1, 8 * BLOCKS), PLANE_GROUPS)
    terms = jnp.sum(terms, axis=0)
    whole = lax.all_to_all(
        jnp.broadcast_to(terms[None], (BLOCKS, 1, 8 * BLOCKS)), "dom", 0, 0, tiled=True
    )
    whole = whole.reshape(8, 2, 2, 4, 4, 2, BLOCKS).transpose(5, 2, 1, 0, 3, 4, 6)
    whole = whole.reshape(2, 2, 2, BLOCKS, BLOCKS)
    whole = jnp.where(core == 0, whole, whole[:, :, ::-1])
    whole = whole.reshape(2, 4 * BLOCKS, BLOCKS)
    lower = jnp.where(z_hi == 0, rotated_near, rotated_far)
    upper = jnp.where(z_hi == 0, rotated_far, rotated_near)
    rotated = jnp.concatenate([lower, upper], axis=0).reshape(1, BX, BY, BZ, width)
    return (rotated, whole[0], whole[1])


def solution(mesh):
    in_specs = (
        P("dom", None, None, None, "band"),
        P("dom", None, None, None),
        P(),
        P(None, "band"),
    )
    out_specs = (P("dom", None, None, None, "band"), P(None, "band"), P(None, "band"))
    return jax.shard_map(local, mesh=mesh, in_specs=in_specs, out_specs=out_specs, check_vma=False)
```

```python
import jax
import jax.numpy as jnp
from jax import lax
from jax.experimental import pallas as pl
from jax.experimental.pallas import tpu as pltpu
from jax.sharding import PartitionSpec as P

STENCIL = (
    -5369.0 / 1800.0,
    12.0 / 7.0,
    -15.0 / 56.0,
    10.0 / 189.0,
    -1.0 / 112.0,
    2.0 / 1925.0,
    -1.0 / 16632.0,
)
REACH = 6
KINETIC = -0.5 / 0.36
BX, BY, BZ = 8, 12, 16
CELLS = BX * BY * BZ
HALF = CELLS // 2
PX, PY, PZ = 4, 4, 8
BLOCKS = PX * PY * PZ
LANES = 128
TILES = CELLS // LANES
HALF_TILES = HALF // LANES
SENT = TILES + HALF_TILES

ORDER = [(ix * PY + iy) * PZ + iz for iz in range(PZ) for iy in range(PY) for ix in range(PX)]
STEP_X, STEP_Y, STEP_Z = 1, PX, PX * PY


def flat(band, dom):
    return band * BLOCKS + dom


def chip(y, x, z):
    return (y * 4 + x) * 4 + z


CORE_GROUPS = [[flat(2 * h + c, d) for d in ORDER for h in range(2)] for c in range(2)]
X_GROUPS = [
    [flat(b, chip(y, x, z)) for x in range(4)]
    for b in range(4)
    for y in range(8)
    for z in range(4)
]
PLANE_GROUPS = [
    [flat(2 * h + c, chip(y, x, z)) for y in range(8) for z in range(4) for h in range(2)]
    for c in range(2)
    for x in range(4)
]
CORE_SWAP = [(0, 1), (1, 0), (2, 3), (3, 2)]
Z_SWAP = [(0, 2), (2, 0), (1, 3), (3, 1)]


def exchange(x, groups):
    return lax.all_to_all(x, ("band", "dom"), 0, 0, tiled=True, axis_index_groups=groups)


OX, OY, OZ = REACH, REACH, 8
EXT = (BX + 2 * REACH, BY + 2 * REACH, BZ + 16, LANES)


def pack_kernel(core_ref, orbitals_ref, potential_ref, out_ref, wide):
    for t in range(TILES):
        tile = orbitals_ref[t * LANES : (t + 1) * LANES]
        out_ref[pl.ds(t, BLOCKS, stride=SENT), :] = jnp.transpose(tile)
    wide[...] = jnp.concatenate([potential_ref[i] for i in range(BX)], axis=1)
    for s in range(HALF_TILES):
        row = wide[pl.ds(core_ref[0] * HALF_TILES + s, 1), :]
        out_ref[pl.ds(TILES + s, BLOCKS, stride=SENT), :] = jnp.broadcast_to(row, (BLOCKS, LANES))


def packed(core, orbitals, potential):
    vmem = pl.BlockSpec(memory_space=pltpu.VMEM)
    return pl.pallas_call(
        pack_kernel,
        out_shape=jax.ShapeDtypeStruct((BLOCKS * SENT, LANES), jnp.float32),
        in_specs=[pl.BlockSpec(memory_space=pltpu.SMEM), vmem, vmem],
        out_specs=vmem,
        scratch_shapes=[pltpu.VMEM((BY, BX * BZ), jnp.float32)],
        compiler_params=pltpu.CompilerParams(vmem_limit_bytes=16 * 1024 * 1024),
    )(core, orbitals, potential)


def split_kernel(got_ref, phi_ref, both_ref):
    for m in range(2):
        for h in range(2):
            for t in range(HALF_TILES):
                tile = got_ref[pl.ds(h * TILES + m * HALF_TILES + t, BLOCKS, stride=2 * TILES), :]
                cells = slice(t * LANES, (t + 1) * LANES)
                at = (2 * m + h) * BLOCKS
                both_ref[at : at + BLOCKS, cells] = tile
                if m == 0:
                    phi_ref[at : at + BLOCKS, cells] = tile


def split_fields(got):
    vmem = pl.BlockSpec(memory_space=pltpu.VMEM)
    return pl.pallas_call(
        split_kernel,
        out_shape=(
            jax.ShapeDtypeStruct((2 * BLOCKS, HALF), jnp.float32),
            jax.ShapeDtypeStruct((4 * BLOCKS, HALF), jnp.float32),
        ),
        in_specs=[vmem],
        out_specs=(vmem, vmem),
        compiler_params=pltpu.CompilerParams(vmem_limit_bytes=16 * 1024 * 1024),
    )(got)


def margins(ext):
    lane = lax.broadcasted_iota(jnp.int32, (1, LANES), 1)
    iz, iy, ix = lane // STEP_Z, lane // STEP_Y % PY, lane // STEP_X % PX
    own_y, own_z = slice(OY, OY + BY), slice(OZ, OZ + BZ)

    def below(v, step, keep):
        return jnp.where(keep, pltpu.roll(v, step, v.ndim - 1), 0.0)

    def above(v, step, keep):
        return jnp.where(keep, pltpu.roll(v, LANES - step, v.ndim - 1), 0.0)

    def inner(i, carry):
        at = i + OX
        ext[at, own_y, 0:8] = below(ext[at, own_y, OZ + 8 : OZ + 16], STEP_Z, iz > 0)
        ext[at, own_y, OZ + BZ : OZ + BZ + 8] = above(ext[at, own_y, OZ : OZ + 8], STEP_Z, iz < PZ - 1)
        ext[at, 0:OY, own_z] = below(ext[at, BY : BY + OY, own_z], STEP_Y, iy > 0)
        ext[at, OY + BY :, own_z] = above(ext[at, OY : 2 * OY, own_z], STEP_Y, iy < PY - 1)
        return carry

    def outer(i, carry):
        ext[i, own_y, own_z] = below(ext[i + BX, own_y, own_z], STEP_X, ix > 0)
        ext[i + OX + BX, own_y, own_z] = above(ext[i + OX, own_y, own_z], STEP_X, ix < PX - 1)
        return carry

    lax.fori_loop(0, BX, inner, 0)
    lax.fori_loop(0, REACH, outer, 0)


YS = BY // 2


def own(ext, i, y0):
    return ext[i + OX, OY + y0 : OY + y0 + YS, OZ : OZ + BZ]


def set_own(ext, i, y0, value):
    ext[i + OX, OY + y0 : OY + y0 + YS, OZ : OZ + BZ] = value


def laplace(ext, i, y0):
    at, y, z = i + OX, OY + y0, OZ
    total = (3.0 * STENCIL[0]) * ext[at, y : y + YS, z : z + BZ]
    for k in range(1, REACH + 1):
        pair_x = ext[at - k, y : y + YS, z : z + BZ] + ext[at + k, y : y + YS, z : z + BZ]
        pair_y = ext[at, y - k : y - k + YS, z : z + BZ] + ext[at, y + k : y + k + YS, z : z + BZ]
        pair_z = ext[at, y : y + YS, z - k : z - k + BZ] + ext[at, y : y + YS, z + k : z + k + BZ]
        total = total + STENCIL[k] * ((pair_x + pair_y) + pair_z)
    return total


def laplace_kernel(got_ref, x_ref, lap_ref, pot_ref, ext):
    for q in range(TILES):
        tile = jnp.transpose(got_ref[pl.ds(q, BLOCKS, stride=SENT), :]).reshape(LANES // BZ, BZ, LANES)
        for r in range(LANES // BZ):
            row = q * (LANES // BZ) + r
            ext[OX + row // BY, OY + row % BY, OZ : OZ + BZ] = tile[r]
            x_ref[row // BY, row % BY] = tile[r]
    for s in range(HALF_TILES):
        tile = jnp.transpose(got_ref[pl.ds(TILES + s, BLOCKS, stride=SENT), :])
        pot_ref[:, s] = tile.reshape(BX, BZ, LANES)
    margins(ext)

    def body(i, carry):
        for y0 in range(0, BY, YS):
            lap_ref[i, y0 : y0 + YS] = laplace(ext, i, y0)
        return carry

    lax.fori_loop(0, BX, body, 0)


def filter_kernel(coef_ref, x_ref, lap_ref, pot_own_ref, v_other_ref, out_ref, ea, eb, pot, img):
    second = coef_ref[7] > 0.5
    for s in range(HALF_TILES):
        other = jnp.transpose(v_other_ref[pl.ds(s, BLOCKS, stride=HALF_TILES), :]).reshape(BX, BZ, LANES)
        mine = pot_own_ref[:, s]
        pot[:, s] = jnp.where(second, other, mine)
        pot[:, s + HALF_TILES] = jnp.where(second, mine, other)

    def image(total, centre, i, y0, scale, shift):
        local = pot[i, y0 : y0 + YS] - shift
        return (scale * KINETIC) * total + scale * (local * centre)

    def first(i, carry):
        for y0 in range(0, BY, YS):
            total, centre = lap_ref[i, y0 : y0 + YS], x_ref[i, y0 : y0 + YS]
            set_own(eb, i, y0, image(total, centre, i, y0, coef_ref[0], coef_ref[1]))
        return carry

    def next_field(i, carry):
        for y0 in range(0, BY, YS):
            new = image(laplace(eb, i, y0), own(eb, i, y0), i, y0, coef_ref[2], coef_ref[1])
            set_own(ea, i, y0, new - coef_ref[3] * x_ref[i, y0 : y0 + YS])
        return carry

    def last_field(i, squares):
        for y0 in range(0, BY, YS):
            new = image(laplace(ea, i, y0), own(ea, i, y0), i, y0, coef_ref[4], coef_ref[1])
            new = new - coef_ref[5] * own(eb, i, y0)
            set_own(eb, i, y0, new)
            squares = squares + jnp.sum(new * new, axis=0)
        return squares

    def image_field(i, carry):
        for y0 in range(0, BY, YS):
            img[i, y0 : y0 + YS] = image(laplace(eb, i, y0), own(eb, i, y0), i, y0, 1.0, 0.0)
        return carry

    lax.fori_loop(0, BX, first, 0)
    margins(eb)
    lax.fori_loop(0, BX, next_field, 0)
    margins(ea)
    squares = lax.fori_loop(0, BX, last_field, jnp.zeros((BZ, LANES), jnp.float32))
    margins(eb)
    lax.fori_loop(0, BX, image_field, 0)
    norm = jnp.sqrt(jnp.sum(squares, keepdims=True))
    for q in range(TILES):
        rows = [q * (LANES // BZ) + r for r in range(LANES // BZ)]
        at = q // HALF_TILES * TILES + q % HALF_TILES
        field = jnp.concatenate([eb[OX + r // BY, OY + r % BY, OZ : OZ + BZ] for r in rows], 0)
        out_ref[pl.ds(at, BLOCKS, stride=2 * TILES), :] = jnp.transpose(field / norm)
        field = jnp.concatenate([img[r // BY, r % BY] for r in rows], 0)
        out_ref[pl.ds(at + HALF_TILES, BLOCKS, stride=2 * TILES), :] = jnp.transpose(field / norm)


FIELD = (BX, BY, BZ, LANES)


def first_laplace(got):
    vmem = pl.BlockSpec(memory_space=pltpu.VMEM)
    return pl.pallas_call(
        laplace_kernel,
        out_shape=(
            jax.ShapeDtypeStruct(FIELD, jnp.float32),
            jax.ShapeDtypeStruct(FIELD, jnp.float32),
            jax.ShapeDtypeStruct((BX, HALF_TILES, BZ, LANES), jnp.float32),
        ),
        in_specs=[vmem],
        out_specs=(vmem, vmem, vmem),
        scratch_shapes=[pltpu.VMEM(EXT, jnp.float32)],
        compiler_params=pltpu.CompilerParams(vmem_limit_bytes=24 * 1024 * 1024),
        cost_estimate=pl.CostEstimate(flops=20_000_000, bytes_accessed=20_000_000, transcendentals=0),
    )(got)


def filtered_fields(coef, x, lap, pot_own, v_other):
    vmem = pl.BlockSpec(memory_space=pltpu.VMEM)
    return pl.pallas_call(
        filter_kernel,
        out_shape=jax.ShapeDtypeStruct((BLOCKS * 2 * TILES, LANES), jnp.float32),
        in_specs=[pl.BlockSpec(memory_space=pltpu.SMEM), vmem, vmem, vmem, vmem],
        out_specs=vmem,
        scratch_shapes=[
            pltpu.VMEM(EXT, jnp.float32),
            pltpu.VMEM(EXT, jnp.float32),
            pltpu.VMEM(FIELD, jnp.float32),
            pltpu.VMEM(FIELD, jnp.float32),
        ],
        compiler_params=pltpu.CompilerParams(vmem_limit_bytes=36 * 1024 * 1024),
        cost_estimate=pl.CostEstimate(flops=60_000_000, bytes_accessed=40_000_000, transcendentals=0),
    )(coef, x, lap, pot_own, v_other)


def filter_coefficients(bounds, second):
    lowest, cutoff, highest = bounds[0], bounds[1], bounds[2]
    half_width = (highest - cutoff) / 2.0
    centre = (highest + cutoff) / 2.0
    s1 = half_width / (lowest - centre)
    tau = 2.0 / s1
    s2 = 1.0 / (tau - s1)
    s3 = 1.0 / (tau - s2)
    return jnp.stack(
        [
            s1 / half_width,
            centre,
            2.0 * s2 / half_width,
            s1 * s2,
            2.0 * s3 / half_width,
            s2 * s3,
            jnp.float32(0.0),
            second,
        ]
    )


def contract(left, right, dims):
    return lax.dot_general(
        left,
        right,
        (dims, ((), ())),
        precision=lax.Precision.HIGH,
        preferred_element_type=jnp.float32,
    )


def local(orbitals, potential, bounds, rotation):
    width = rotation.shape[1]
    band = lax.axis_index("band")
    z_hi, core = band // 2, band % 2
    coef = filter_coefficients(bounds, core.astype(jnp.float32))

    sent = packed(core.reshape(1), orbitals.reshape(CELLS, width), potential[0])
    got = lax.all_to_all(
        sent.reshape(BLOCKS, 1, SENT * LANES), "dom", 0, 0, tiled=True, axis_index_groups=[ORDER]
    )
    got, rotation_near = lax.optimization_barrier((got, rotation))
    rotation_far = lax.ppermute(rotation_near, "band", Z_SWAP)
    v_other = lax.ppermute(got[:, :, CELLS:], "band", CORE_SWAP)
    x, lap, pot_own = first_laplace(got.reshape(BLOCKS * SENT, LANES))
    images = filtered_fields(coef, x, lap, pot_own, v_other.reshape(BLOCKS * HALF_TILES, LANES))

    images, rotation_far = lax.optimization_barrier((images, rotation_far))
    got = exchange(images.reshape(2 * BLOCKS, 1, CELLS), CORE_GROUPS)
    got, rotation_near, rotation_far = lax.optimization_barrier((got, rotation_near, rotation_far))
    phi, both = split_fields(got.reshape(2 * BLOCKS * TILES, LANES))
    phi_other = lax.ppermute(phi, "band", CORE_SWAP)
    gram = jnp.concatenate(
        [contract(phi, both, ((1,), (1,))), contract(phi_other, both, ((1,), (1,)))], axis=0
    )

    def by_core(weights):
        weights = weights.reshape(2, 2, BLOCKS, width)
        swapped = jnp.where(core == 0, weights, weights[:, ::-1])
        return swapped.transpose(1, 0, 2, 3).reshape(4 * BLOCKS, width)

    def rotate(weights, start, end):
        cells = slice(start, end)
        return contract(phi[:, cells], weights[: 2 * BLOCKS], ((0,), (0,))) + contract(
            phi_other[:, cells], weights[2 * BLOCKS :], ((0,), (0,))
        )

    far = by_core(rotation_far)
    cuts = (0, HALF // 2, 5 * HALF // 6, HALF)
    parts = []

    def send_part(k, tie):
        tie, part = lax.optimization_barrier((tie, rotate(far, cuts[k], cuts[k + 1])))
        parts.append(lax.ppermute(part, "band", Z_SWAP))
        return tie

    gram = send_part(0, gram)
    terms = exchange(gram.reshape(4, BLOCKS, 4 * BLOCKS), X_GROUPS)
    terms, parts[0] = lax.optimization_barrier((terms, parts[0]))
    terms = jnp.sum(terms, axis=0)
    terms = terms.reshape(32, 4, 2, 2, BLOCKS).transpose(0, 3, 1, 2, 4).reshape(64, 8 * BLOCKS)
    terms = send_part(1, terms)
    terms = exchange(terms.reshape(64, 1, 8 * BLOCKS), PLANE_GROUPS)
    terms, parts[1] = lax.optimization_barrier((terms, parts[1]))
    terms = send_part(2, jnp.sum(terms, axis=0))
    whole = lax.all_to_all(
        jnp.broadcast_to(terms[None], (BLOCKS, 1, 8 * BLOCKS)), "dom", 0, 0, tiled=True
    )
    whole = whole.reshape(8, 2, 2, 4, 4, 2, BLOCKS).transpose(5, 2, 1, 0, 3, 4, 6)
    whole = whole.reshape(2, 2, 2, BLOCKS, BLOCKS)
    whole = jnp.where(core == 0, whole, whole[:, :, ::-1])
    whole = whole.reshape(2, 4 * BLOCKS, BLOCKS)
    rotated_near = rotate(by_core(rotation_near), 0, HALF)
    rotated_far = jnp.concatenate(parts, axis=0)
    lower = jnp.where(z_hi == 0, rotated_near, rotated_far)
    upper = jnp.where(z_hi == 0, rotated_far, rotated_near)
    rotated = jnp.concatenate([lower, upper], axis=0).reshape(1, BX, BY, BZ, width)
    return (rotated, whole[0], whole[1])


def solution(mesh):
    in_specs = (
        P("dom", None, None, None, "band"),
        P("dom", None, None, None),
        P(),
        P(None, "band"),
    )
    out_specs = (P("dom", None, None, None, "band"), P(None, "band"), P(None, "band"))
    return jax.shard_map(local, mesh=mesh, in_specs=in_specs, out_specs=out_specs, check_vma=False)
```

```python
import jax
import jax.numpy as jnp
from jax import lax
from jax.experimental import pallas as pl
from jax.experimental.pallas import tpu as pltpu
from jax.sharding import PartitionSpec as P

STENCIL = (
    -5369.0 / 1800.0,
    12.0 / 7.0,
    -15.0 / 56.0,
    10.0 / 189.0,
    -1.0 / 112.0,
    2.0 / 1925.0,
    -1.0 / 16632.0,
)
REACH = 6
KINETIC = -0.5 / 0.36
BX, BY, BZ = 8, 12, 16
CELLS = BX * BY * BZ
HALF = CELLS // 2
PX, PY, PZ = 4, 4, 8
BLOCKS = PX * PY * PZ
LANES = 128
TILES = CELLS // LANES
HALF_TILES = HALF // LANES
SENT = TILES + HALF_TILES

ORDER = [(ix * PY + iy) * PZ + iz for iz in range(PZ) for iy in range(PY) for ix in range(PX)]
STEP_X, STEP_Y, STEP_Z = 1, PX, PX * PY


def flat(band, dom):
    return band * BLOCKS + dom


def chip(y, x, z):
    return (y * 4 + x) * 4 + z


CORE_GROUPS = [[flat(2 * h + c, d) for d in ORDER for h in range(2)] for c in range(2)]
PLANE_GROUPS = [
    [flat(2 * h + c, chip(y, x, z)) for y in range(8) for z in range(4) for h in range(2)]
    for c in range(2)
    for x in range(4)
]
CORE_SWAP = [(0, 1), (1, 0), (2, 3), (3, 2)]
Z_SWAP = [(0, 2), (2, 0), (1, 3), (3, 1)]


def exchange(x, groups):
    return lax.all_to_all(x, ("band", "dom"), 0, 0, tiled=True, axis_index_groups=groups)


OX, OY, OZ = REACH, REACH, 8
EXT = (BX + 2 * REACH, BY + 2 * REACH, BZ + 16, LANES)


def pack_kernel(core_ref, orbitals_ref, potential_ref, out_ref, wide):
    for t in range(TILES):
        tile = orbitals_ref[t * LANES : (t + 1) * LANES]
        out_ref[pl.ds(t, BLOCKS, stride=SENT), :] = jnp.transpose(tile)
    wide[...] = jnp.concatenate([potential_ref[i] for i in range(BX)], axis=1)
    for s in range(HALF_TILES):
        row = wide[pl.ds(core_ref[0] * HALF_TILES + s, 1), :]
        out_ref[pl.ds(TILES + s, BLOCKS, stride=SENT), :] = jnp.broadcast_to(row, (BLOCKS, LANES))


def packed(core, orbitals, potential):
    vmem = pl.BlockSpec(memory_space=pltpu.VMEM)
    return pl.pallas_call(
        pack_kernel,
        out_shape=jax.ShapeDtypeStruct((BLOCKS * SENT, LANES), jnp.float32),
        in_specs=[pl.BlockSpec(memory_space=pltpu.SMEM), vmem, vmem],
        out_specs=vmem,
        scratch_shapes=[pltpu.VMEM((BY, BX * BZ), jnp.float32)],
        compiler_params=pltpu.CompilerParams(vmem_limit_bytes=16 * 1024 * 1024),
    )(core, orbitals, potential)


def split_kernel(got_ref, phi_ref, both_ref):
    for m in range(2):
        for h in range(2):
            for t in range(HALF_TILES):
                tile = got_ref[pl.ds(h * TILES + m * HALF_TILES + t, BLOCKS, stride=2 * TILES), :]
                cells = slice(t * LANES, (t + 1) * LANES)
                at = (2 * m + h) * BLOCKS
                both_ref[at : at + BLOCKS, cells] = tile
                if m == 0:
                    phi_ref[at : at + BLOCKS, cells] = tile


def split_fields(got):
    vmem = pl.BlockSpec(memory_space=pltpu.VMEM)
    return pl.pallas_call(
        split_kernel,
        out_shape=(
            jax.ShapeDtypeStruct((2 * BLOCKS, HALF), jnp.float32),
            jax.ShapeDtypeStruct((4 * BLOCKS, HALF), jnp.float32),
        ),
        in_specs=[vmem],
        out_specs=(vmem, vmem),
        compiler_params=pltpu.CompilerParams(vmem_limit_bytes=16 * 1024 * 1024),
    )(got)


def margins(ext):
    lane = lax.broadcasted_iota(jnp.int32, (1, LANES), 1)
    iz, iy, ix = lane // STEP_Z, lane // STEP_Y % PY, lane // STEP_X % PX
    own_y, own_z = slice(OY, OY + BY), slice(OZ, OZ + BZ)

    def below(v, step, keep):
        return jnp.where(keep, pltpu.roll(v, step, v.ndim - 1), 0.0)

    def above(v, step, keep):
        return jnp.where(keep, pltpu.roll(v, LANES - step, v.ndim - 1), 0.0)

    def inner(i, carry):
        at = i + OX
        ext[at, own_y, 0:8] = below(ext[at, own_y, OZ + 8 : OZ + 16], STEP_Z, iz > 0)
        ext[at, own_y, OZ + BZ : OZ + BZ + 8] = above(ext[at, own_y, OZ : OZ + 8], STEP_Z, iz < PZ - 1)
        ext[at, 0:OY, own_z] = below(ext[at, BY : BY + OY, own_z], STEP_Y, iy > 0)
        ext[at, OY + BY :, own_z] = above(ext[at, OY : 2 * OY, own_z], STEP_Y, iy < PY - 1)
        return carry

    def outer(i, carry):
        ext[i, own_y, own_z] = below(ext[i + BX, own_y, own_z], STEP_X, ix > 0)
        ext[i + OX + BX, own_y, own_z] = above(ext[i + OX, own_y, own_z], STEP_X, ix < PX - 1)
        return carry

    lax.fori_loop(0, BX, inner, 0)
    lax.fori_loop(0, REACH, outer, 0)


YS = BY // 2


def own(ext, i, y0):
    return ext[i + OX, OY + y0 : OY + y0 + YS, OZ : OZ + BZ]


def set_own(ext, i, y0, value):
    ext[i + OX, OY + y0 : OY + y0 + YS, OZ : OZ + BZ] = value


def laplace(ext, i, y0):
    at, y, z = i + OX, OY + y0, OZ
    total = (3.0 * STENCIL[0]) * ext[at, y : y + YS, z : z + BZ]
    for k in range(1, REACH + 1):
        pair_x = ext[at - k, y : y + YS, z : z + BZ] + ext[at + k, y : y + YS, z : z + BZ]
        pair_y = ext[at, y - k : y - k + YS, z : z + BZ] + ext[at, y + k : y + k + YS, z : z + BZ]
        pair_z = ext[at, y : y + YS, z - k : z - k + BZ] + ext[at, y : y + YS, z + k : z + k + BZ]
        total = total + STENCIL[k] * ((pair_x + pair_y) + pair_z)
    return total


def laplace_kernel(got_ref, x_ref, lap_ref, pot_ref, ext):
    for q in range(TILES):
        tile = jnp.transpose(got_ref[pl.ds(q, BLOCKS, stride=SENT), :]).reshape(LANES // BZ, BZ, LANES)
        for r in range(LANES // BZ):
            row = q * (LANES // BZ) + r
            ext[OX + row // BY, OY + row % BY, OZ : OZ + BZ] = tile[r]
            x_ref[row // BY, row % BY] = tile[r]
    for s in range(HALF_TILES):
        tile = jnp.transpose(got_ref[pl.ds(TILES + s, BLOCKS, stride=SENT), :])
        pot_ref[:, s] = tile.reshape(BX, BZ, LANES)
    margins(ext)

    def body(i, carry):
        for y0 in range(0, BY, YS):
            lap_ref[i, y0 : y0 + YS] = laplace(ext, i, y0)
        return carry

    lax.fori_loop(0, BX, body, 0)


def filter_kernel(coef_ref, x_ref, lap_ref, pot_own_ref, v_other_ref, out_ref, ea, eb, pot, img):
    second = coef_ref[7] > 0.5
    for s in range(HALF_TILES):
        other = jnp.transpose(v_other_ref[pl.ds(s, BLOCKS, stride=HALF_TILES), :]).reshape(BX, BZ, LANES)
        mine = pot_own_ref[:, s]
        pot[:, s] = jnp.where(second, other, mine)
        pot[:, s + HALF_TILES] = jnp.where(second, mine, other)

    def image(total, centre, i, y0, scale, shift):
        local = pot[i, y0 : y0 + YS] - shift
        return (scale * KINETIC) * total + scale * (local * centre)

    def first(i, carry):
        for y0 in range(0, BY, YS):
            total, centre = lap_ref[i, y0 : y0 + YS], x_ref[i, y0 : y0 + YS]
            set_own(eb, i, y0, image(total, centre, i, y0, coef_ref[0], coef_ref[1]))
        return carry

    def next_field(i, carry):
        for y0 in range(0, BY, YS):
            new = image(laplace(eb, i, y0), own(eb, i, y0), i, y0, coef_ref[2], coef_ref[1])
            set_own(ea, i, y0, new - coef_ref[3] * x_ref[i, y0 : y0 + YS])
        return carry

    def last_field(i, squares):
        for y0 in range(0, BY, YS):
            new = image(laplace(ea, i, y0), own(ea, i, y0), i, y0, coef_ref[4], coef_ref[1])
            new = new - coef_ref[5] * own(eb, i, y0)
            set_own(eb, i, y0, new)
            squares = squares + jnp.sum(new * new, axis=0)
        return squares

    def image_field(i, carry):
        for y0 in range(0, BY, YS):
            img[i, y0 : y0 + YS] = image(laplace(eb, i, y0), own(eb, i, y0), i, y0, 1.0, 0.0)
        return carry

    lax.fori_loop(0, BX, first, 0)
    margins(eb)
    lax.fori_loop(0, BX, next_field, 0)
    margins(ea)
    squares = lax.fori_loop(0, BX, last_field, jnp.zeros((BZ, LANES), jnp.float32))
    margins(eb)
    lax.fori_loop(0, BX, image_field, 0)
    norm = jnp.sqrt(jnp.sum(squares, keepdims=True))
    for q in range(TILES):
        rows = [q * (LANES // BZ) + r for r in range(LANES // BZ)]
        at = q // HALF_TILES * TILES + q % HALF_TILES
        field = jnp.concatenate([eb[OX + r // BY, OY + r % BY, OZ : OZ + BZ] for r in rows], 0)
        out_ref[pl.ds(at, BLOCKS, stride=2 * TILES), :] = jnp.transpose(field / norm)
        field = jnp.concatenate([img[r // BY, r % BY] for r in rows], 0)
        out_ref[pl.ds(at + HALF_TILES, BLOCKS, stride=2 * TILES), :] = jnp.transpose(field / norm)


FIELD = (BX, BY, BZ, LANES)


def first_laplace(got):
    vmem = pl.BlockSpec(memory_space=pltpu.VMEM)
    return pl.pallas_call(
        laplace_kernel,
        out_shape=(
            jax.ShapeDtypeStruct(FIELD, jnp.float32),
            jax.ShapeDtypeStruct(FIELD, jnp.float32),
            jax.ShapeDtypeStruct((BX, HALF_TILES, BZ, LANES), jnp.float32),
        ),
        in_specs=[vmem],
        out_specs=(vmem, vmem, vmem),
        scratch_shapes=[pltpu.VMEM(EXT, jnp.float32)],
        compiler_params=pltpu.CompilerParams(vmem_limit_bytes=24 * 1024 * 1024),
        cost_estimate=pl.CostEstimate(flops=20_000_000, bytes_accessed=20_000_000, transcendentals=0),
    )(got)


def filtered_fields(coef, x, lap, pot_own, v_other):
    vmem = pl.BlockSpec(memory_space=pltpu.VMEM)
    return pl.pallas_call(
        filter_kernel,
        out_shape=jax.ShapeDtypeStruct((BLOCKS * 2 * TILES, LANES), jnp.float32),
        in_specs=[pl.BlockSpec(memory_space=pltpu.SMEM), vmem, vmem, vmem, vmem],
        out_specs=vmem,
        scratch_shapes=[
            pltpu.VMEM(EXT, jnp.float32),
            pltpu.VMEM(EXT, jnp.float32),
            pltpu.VMEM(FIELD, jnp.float32),
            pltpu.VMEM(FIELD, jnp.float32),
        ],
        compiler_params=pltpu.CompilerParams(vmem_limit_bytes=36 * 1024 * 1024),
        cost_estimate=pl.CostEstimate(flops=60_000_000, bytes_accessed=40_000_000, transcendentals=0),
    )(coef, x, lap, pot_own, v_other)


def filter_coefficients(bounds, second):
    lowest, cutoff, highest = bounds[0], bounds[1], bounds[2]
    half_width = (highest - cutoff) / 2.0
    centre = (highest + cutoff) / 2.0
    s1 = half_width / (lowest - centre)
    tau = 2.0 / s1
    s2 = 1.0 / (tau - s1)
    s3 = 1.0 / (tau - s2)
    return jnp.stack(
        [
            s1 / half_width,
            centre,
            2.0 * s2 / half_width,
            s1 * s2,
            2.0 * s3 / half_width,
            s2 * s3,
            jnp.float32(0.0),
            second,
        ]
    )


def contract(left, right, dims):
    return lax.dot_general(
        left,
        right,
        (dims, ((), ())),
        precision=lax.Precision.HIGH,
        preferred_element_type=jnp.float32,
    )


def local(orbitals, potential, bounds, rotation):
    width = rotation.shape[1]
    band = lax.axis_index("band")
    z_hi, core = band // 2, band % 2
    coef = filter_coefficients(bounds, core.astype(jnp.float32))

    sent = packed(core.reshape(1), orbitals.reshape(CELLS, width), potential[0])
    got = lax.all_to_all(
        sent.reshape(BLOCKS, 1, SENT * LANES), "dom", 0, 0, tiled=True, axis_index_groups=[ORDER]
    )
    got, rotation_near = lax.optimization_barrier((got, rotation))
    rotation_far = lax.ppermute(rotation_near, "band", Z_SWAP)
    v_other = lax.ppermute(got[:, :, CELLS:], "band", CORE_SWAP)
    x, lap, pot_own = first_laplace(got.reshape(BLOCKS * SENT, LANES))
    images = filtered_fields(coef, x, lap, pot_own, v_other.reshape(BLOCKS * HALF_TILES, LANES))

    images, rotation_far = lax.optimization_barrier((images, rotation_far))
    got = exchange(images.reshape(2 * BLOCKS, 1, CELLS), CORE_GROUPS)
    got, rotation_near, rotation_far = lax.optimization_barrier((got, rotation_near, rotation_far))
    phi, both = split_fields(got.reshape(2 * BLOCKS * TILES, LANES))
    phi_other = lax.ppermute(phi, "band", CORE_SWAP)
    gram = jnp.concatenate(
        [contract(phi, both, ((1,), (1,))), contract(phi_other, both, ((1,), (1,)))], axis=0
    )

    def by_core(weights):
        weights = weights.reshape(2, 2, BLOCKS, width)
        swapped = jnp.where(core == 0, weights, weights[:, ::-1])
        return swapped.transpose(1, 0, 2, 3).reshape(4 * BLOCKS, width)

    def rotate(weights):
        weights = by_core(weights)
        return contract(phi, weights[: 2 * BLOCKS], ((0,), (0,))) + contract(
            phi_other, weights[2 * BLOCKS :], ((0,), (0,))
        )

    rotated_far = lax.ppermute(rotate(rotation_far), "band", Z_SWAP)

    gram = gram.reshape(4, BLOCKS, 4 * BLOCKS)
    place = lax.axis_index("dom") // 4 % 4
    pieces = [lax.dynamic_index_in_dim(gram, (place + k) % 4, 0, keepdims=False) for k in range(4)]
    for k in (2, 1, 3):
        pairs = [
            (chip(y, x, z), chip(y, (x + k) % 4, z)) for y in range(8) for x in range(4) for z in range(4)
        ]
        pieces[k] = lax.ppermute(pieces[k], "dom", pairs)
    terms, rotated_far = lax.optimization_barrier((pieces, rotated_far))
    terms = (terms[0] + terms[1]) + (terms[2] + terms[3])
    terms = terms.reshape(32, 4, 2, 2, BLOCKS).transpose(0, 3, 1, 2, 4).reshape(64, 8 * BLOCKS)
    terms = exchange(terms.reshape(64, 1, 8 * BLOCKS), PLANE_GROUPS)
    terms = jnp.sum(terms, axis=0)
    whole = lax.all_to_all(
        jnp.broadcast_to(terms[None], (BLOCKS, 1, 8 * BLOCKS)), "dom", 0, 0, tiled=True
    )
    whole = whole.reshape(8, 2, 2, 4, 4, 2, BLOCKS).transpose(5, 2, 1, 0, 3, 4, 6)
    whole = whole.reshape(2, 2, 2, BLOCKS, BLOCKS)
    whole = jnp.where(core == 0, whole, whole[:, :, ::-1])
    whole = whole.reshape(2, 4 * BLOCKS, BLOCKS)
    rotated_near = rotate(rotation_near)
    lower = jnp.where(z_hi == 0, rotated_near, rotated_far)
    upper = jnp.where(z_hi == 0, rotated_far, rotated_near)
    rotated = jnp.concatenate([lower, upper], axis=0).reshape(1, BX, BY, BZ, width)
    return (rotated, whole[0], whole[1])


def solution(mesh):
    in_specs = (
        P("dom", None, None, None, "band"),
        P("dom", None, None, None),
        P(),
        P(None, "band"),
    )
    out_specs = (P("dom", None, None, None, "band"), P(None, "band"), P(None, "band"))
    return jax.shard_map(local, mesh=mesh, in_specs=in_specs, out_specs=out_specs, check_vma=False)
```

```python
import jax
import jax.numpy as jnp
from jax import lax
from jax.experimental import pallas as pl
from jax.experimental.pallas import tpu as pltpu
from jax.sharding import PartitionSpec as P

STENCIL = (
    -5369.0 / 1800.0,
    12.0 / 7.0,
    -15.0 / 56.0,
    10.0 / 189.0,
    -1.0 / 112.0,
    2.0 / 1925.0,
    -1.0 / 16632.0,
)
REACH = 6
KINETIC = -0.5 / 0.36
BX, BY, BZ = 8, 12, 16
CELLS = BX * BY * BZ
HALF = CELLS // 2
PX, PY, PZ = 4, 4, 8
BLOCKS = PX * PY * PZ
LANES = 128
TILES = CELLS // LANES
HALF_TILES = HALF // LANES
SENT = TILES + HALF_TILES

ORDER = [(ix * PY + iy) * PZ + iz for iz in range(PZ) for iy in range(PY) for ix in range(PX)]
STEP_X, STEP_Y, STEP_Z = 1, PX, PX * PY


def flat(band, dom):
    return band * BLOCKS + dom


def chip(y, x, z):
    return (y * 4 + x) * 4 + z


CORE_GROUPS = [[flat(2 * h + c, d) for d in ORDER for h in range(2)] for c in range(2)]
PLANE_GROUPS = [
    [flat(2 * h + c, chip(y, x, z)) for y in range(8) for z in range(4) for h in range(2)]
    for c in range(2)
    for x in range(4)
]
CORE_SWAP = [(0, 1), (1, 0), (2, 3), (3, 2)]
Z_SWAP = [(0, 2), (2, 0), (1, 3), (3, 1)]


def exchange(x, groups):
    return lax.all_to_all(x, ("band", "dom"), 0, 0, tiled=True, axis_index_groups=groups)


OX, OY, OZ = REACH, REACH, 8
EXT = (BX + 2 * REACH, BY + 2 * REACH, BZ + 16, LANES)


def pack_kernel(core_ref, orbitals_ref, potential_ref, out_ref, wide):
    for t in range(TILES):
        tile = orbitals_ref[t * LANES : (t + 1) * LANES]
        out_ref[pl.ds(t, BLOCKS, stride=SENT), :] = jnp.transpose(tile)
    wide[...] = jnp.concatenate([potential_ref[i] for i in range(BX)], axis=1)
    for s in range(HALF_TILES):
        row = wide[pl.ds(core_ref[0] * HALF_TILES + s, 1), :]
        out_ref[pl.ds(TILES + s, BLOCKS, stride=SENT), :] = jnp.broadcast_to(row, (BLOCKS, LANES))


def packed(core, orbitals, potential):
    vmem = pl.BlockSpec(memory_space=pltpu.VMEM)
    return pl.pallas_call(
        pack_kernel,
        out_shape=jax.ShapeDtypeStruct((BLOCKS * SENT, LANES), jnp.float32),
        in_specs=[pl.BlockSpec(memory_space=pltpu.SMEM), vmem, vmem],
        out_specs=vmem,
        scratch_shapes=[pltpu.VMEM((BY, BX * BZ), jnp.float32)],
        compiler_params=pltpu.CompilerParams(vmem_limit_bytes=16 * 1024 * 1024),
    )(core, orbitals, potential)


def split_kernel(got_ref, phi_ref, both_ref):
    for m in range(2):
        for h in range(2):
            for t in range(HALF_TILES):
                tile = got_ref[pl.ds(h * TILES + m * HALF_TILES + t, BLOCKS, stride=2 * TILES), :]
                cells = slice(t * LANES, (t + 1) * LANES)
                at = (2 * m + h) * BLOCKS
                both_ref[at : at + BLOCKS, cells] = tile
                if m == 0:
                    phi_ref[at : at + BLOCKS, cells] = tile


def split_fields(got):
    vmem = pl.BlockSpec(memory_space=pltpu.VMEM)
    return pl.pallas_call(
        split_kernel,
        out_shape=(
            jax.ShapeDtypeStruct((2 * BLOCKS, HALF), jnp.float32),
            jax.ShapeDtypeStruct((4 * BLOCKS, HALF), jnp.float32),
        ),
        in_specs=[vmem],
        out_specs=(vmem, vmem),
        compiler_params=pltpu.CompilerParams(vmem_limit_bytes=16 * 1024 * 1024),
    )(got)


def margins(ext):
    lane = lax.broadcasted_iota(jnp.int32, (8, LANES), 1)
    iz, iy, ix = lane // STEP_Z, lane // STEP_Y % PY, lane // STEP_X % PX
    masks = {0: (ix > 0, ix < PX - 1), 1: (iy > 0, iy < PY - 1), 2: (iz > 0, iz < PZ - 1)}
    steps = (STEP_X, STEP_Y, STEP_Z)

    def carry(dim, to_below, to_above, from_below, from_above):
        below, above = masks[dim]
        ext[to_below] = jnp.where(below, pltpu.roll(ext[from_below], steps[dim], 1), 0.0)
        ext[to_above] = jnp.where(above, pltpu.roll(ext[from_above], LANES - steps[dim], 1), 0.0)

    def at(x, y, z):
        return (x, y, slice(z, z + 8))

    for x in range(OX, OX + BX):
        for y in range(OY, OY + BY):
            carry(2, at(x, y, OZ - 8), at(x, y, OZ + BZ), at(x, y, OZ + BZ - 8), at(x, y, OZ))
        for y in range(OY):
            for z in range(OZ, OZ + BZ, 8):
                carry(1, at(x, y, z), at(x, y + OY + BY, z), at(x, y + BY, z), at(x, y + OY, z))
    for x in range(OX):
        for y in range(OY, OY + BY):
            for z in range(OZ, OZ + BZ, 8):
                carry(0, at(x, y, z), at(x + OX + BX, y, z), at(x + BX, y, z), at(x + OX, y, z))


YS = BY // 2


def own(ext, i, y0):
    return ext[i + OX, OY + y0 : OY + y0 + YS, OZ : OZ + BZ]


def set_own(ext, i, y0, value):
    ext[i + OX, OY + y0 : OY + y0 + YS, OZ : OZ + BZ] = value


def laplace(ext, i, y0):
    at, y, z = i + OX, OY + y0, OZ
    total = (3.0 * STENCIL[0]) * ext[at, y : y + YS, z : z + BZ]
    for k in range(1, REACH + 1):
        pair_x = ext[at - k, y : y + YS, z : z + BZ] + ext[at + k, y : y + YS, z : z + BZ]
        pair_y = ext[at, y - k : y - k + YS, z : z + BZ] + ext[at, y + k : y + k + YS, z : z + BZ]
        pair_z = ext[at, y : y + YS, z - k : z - k + BZ] + ext[at, y : y + YS, z + k : z + k + BZ]
        total = total + STENCIL[k] * ((pair_x + pair_y) + pair_z)
    return total


def laplace_kernel(got_ref, x_ref, lap_ref, pot_ref, ext):
    for q in range(TILES):
        tile = jnp.transpose(got_ref[pl.ds(q, BLOCKS, stride=SENT), :]).reshape(LANES // BZ, BZ, LANES)
        for r in range(LANES // BZ):
            row = q * (LANES // BZ) + r
            ext[OX + row // BY, OY + row % BY, OZ : OZ + BZ] = tile[r]
            x_ref[row // BY, row % BY] = tile[r]
    for s in range(HALF_TILES):
        tile = jnp.transpose(got_ref[pl.ds(TILES + s, BLOCKS, stride=SENT), :])
        pot_ref[:, s] = tile.reshape(BX, BZ, LANES)
    margins(ext)

    def body(i, carry):
        for y0 in range(0, BY, YS):
            lap_ref[i, y0 : y0 + YS] = laplace(ext, i, y0)
        return carry

    lax.fori_loop(0, BX, body, 0)


def filter_coefficients(bounds_ref):
    lowest, cutoff, highest = (jnp.full((1, LANES), bounds_ref[k], jnp.float32) for k in range(3))
    half_width = (highest - cutoff) / 2.0
    centre = (highest + cutoff) / 2.0
    s1 = half_width / (lowest - centre)
    tau = 2.0 / s1
    s2 = 1.0 / (tau - s1)
    s3 = 1.0 / (tau - s2)
    scales = (s1 / half_width, 2.0 * s2 / half_width, 2.0 * s3 / half_width)
    return centre, scales, (None, s1 * s2, s2 * s3)


def filter_kernel(core_ref, bounds_ref, x_ref, lap_ref, pot_own_ref, v_other_ref, out_ref, ea, eb, pot, img):
    shift, scales, backs = filter_coefficients(bounds_ref)
    second = core_ref[0] == 1
    for s in range(HALF_TILES):
        other = jnp.transpose(v_other_ref[pl.ds(s, BLOCKS, stride=HALF_TILES), :]).reshape(BX, BZ, LANES)
        mine = pot_own_ref[:, s]
        pot[:, s] = jnp.where(second, other, mine)
        pot[:, s + HALF_TILES] = jnp.where(second, mine, other)

    def image(total, centre, i, y0):
        return KINETIC * total + (pot[i, y0 : y0 + YS] - shift) * centre

    def first(i, carry):
        for y0 in range(0, BY, YS):
            total, centre = lap_ref[i, y0 : y0 + YS], x_ref[i, y0 : y0 + YS]
            set_own(eb, i, y0, scales[0] * image(total, centre, i, y0))
        return carry

    def next_field(i, carry):
        for y0 in range(0, BY, YS):
            new = scales[1] * image(laplace(eb, i, y0), own(eb, i, y0), i, y0)
            set_own(ea, i, y0, new - backs[1] * x_ref[i, y0 : y0 + YS])
        return carry

    def last_field(i, squares):
        for y0 in range(0, BY, YS):
            new = scales[2] * image(laplace(ea, i, y0), own(ea, i, y0), i, y0)
            new = new - backs[2] * own(eb, i, y0)
            set_own(eb, i, y0, new)
            squares = squares + jnp.sum(new * new, axis=0)
        return squares

    def image_field(i, carry):
        for y0 in range(0, BY, YS):
            centre = own(eb, i, y0)
            img[i, y0 : y0 + YS] = KINETIC * laplace(eb, i, y0) + pot[i, y0 : y0 + YS] * centre
        return carry

    lax.fori_loop(0, BX, first, 0)
    margins(eb)
    lax.fori_loop(0, BX, next_field, 0)
    margins(ea)
    squares = lax.fori_loop(0, BX, last_field, jnp.zeros((BZ, LANES), jnp.float32))
    margins(eb)
    lax.fori_loop(0, BX, image_field, 0)
    norm = jnp.sqrt(jnp.sum(squares, keepdims=True))
    for q in range(TILES):
        rows = [q * (LANES // BZ) + r for r in range(LANES // BZ)]
        at = q // HALF_TILES * TILES + q % HALF_TILES
        field = jnp.concatenate([eb[OX + r // BY, OY + r % BY, OZ : OZ + BZ] for r in rows], 0)
        out_ref[pl.ds(at, BLOCKS, stride=2 * TILES), :] = jnp.transpose(field / norm)
        field = jnp.concatenate([img[r // BY, r % BY] for r in rows], 0)
        out_ref[pl.ds(at + HALF_TILES, BLOCKS, stride=2 * TILES), :] = jnp.transpose(field / norm)


FIELD = (BX, BY, BZ, LANES)


def first_laplace(got):
    vmem = pl.BlockSpec(memory_space=pltpu.VMEM)
    return pl.pallas_call(
        laplace_kernel,
        out_shape=(
            jax.ShapeDtypeStruct(FIELD, jnp.float32),
            jax.ShapeDtypeStruct(FIELD, jnp.float32),
            jax.ShapeDtypeStruct((BX, HALF_TILES, BZ, LANES), jnp.float32),
        ),
        in_specs=[vmem],
        out_specs=(vmem, vmem, vmem),
        scratch_shapes=[pltpu.VMEM(EXT, jnp.float32)],
        compiler_params=pltpu.CompilerParams(vmem_limit_bytes=24 * 1024 * 1024),
        cost_estimate=pl.CostEstimate(flops=20_000_000, bytes_accessed=20_000_000, transcendentals=0),
    )(got)


def filtered_fields(core, bounds, x, lap, pot_own, v_other):
    vmem = pl.BlockSpec(memory_space=pltpu.VMEM)
    return pl.pallas_call(
        filter_kernel,
        out_shape=jax.ShapeDtypeStruct((BLOCKS * 2 * TILES, LANES), jnp.float32),
        in_specs=[pl.BlockSpec(memory_space=pltpu.SMEM)] * 2 + [vmem] * 4,
        out_specs=vmem,
        scratch_shapes=[
            pltpu.VMEM(EXT, jnp.float32),
            pltpu.VMEM(EXT, jnp.float32),
            pltpu.VMEM(FIELD, jnp.float32),
            pltpu.VMEM(FIELD, jnp.float32),
        ],
        compiler_params=pltpu.CompilerParams(vmem_limit_bytes=36 * 1024 * 1024),
        cost_estimate=pl.CostEstimate(flops=60_000_000, bytes_accessed=40_000_000, transcendentals=0),
    )(core, bounds, x, lap, pot_own, v_other)


def contract(left, right, dims):
    return lax.dot_general(
        left,
        right,
        (dims, ((), ())),
        precision=lax.Precision.HIGH,
        preferred_element_type=jnp.float32,
    )


def local(orbitals, potential, bounds, rotation):
    width = rotation.shape[1]
    band = lax.axis_index("band")
    z_hi, core = band >> 1, band & 1
    here = core.reshape(1)

    sent = packed(here, orbitals.reshape(CELLS, width), potential[0])
    got = lax.all_to_all(
        sent.reshape(BLOCKS, 1, SENT * LANES), "dom", 0, 0, tiled=True, axis_index_groups=[ORDER]
    )
    got, rotation_near = lax.optimization_barrier((got, rotation))
    rotation_far = lax.ppermute(rotation_near, "band", Z_SWAP)
    v_other = lax.ppermute(got[:, :, CELLS:], "band", CORE_SWAP)
    x, lap, pot_own = first_laplace(got.reshape(BLOCKS * SENT, LANES))
    images = filtered_fields(
        here, bounds, x, lap, pot_own, v_other.reshape(BLOCKS * HALF_TILES, LANES)
    )

    images, rotation_far = lax.optimization_barrier((images, rotation_far))
    got = exchange(images.reshape(2 * BLOCKS, 1, CELLS), CORE_GROUPS)
    got, rotation_near, rotation_far = lax.optimization_barrier((got, rotation_near, rotation_far))
    phi, both = split_fields(got.reshape(2 * BLOCKS * TILES, LANES))
    phi_other = lax.ppermute(phi, "band", CORE_SWAP)
    gram = jnp.concatenate(
        [contract(phi, both, ((1,), (1,))), contract(phi_other, both, ((1,), (1,)))], axis=0
    )

    def by_core(weights):
        weights = weights.reshape(2, 2, BLOCKS, width)
        swapped = jnp.where(core == 0, weights, weights[:, ::-1])
        return swapped.transpose(1, 0, 2, 3).reshape(4 * BLOCKS, width)

    def rotate(weights):
        weights = by_core(weights)
        return contract(phi, weights[: 2 * BLOCKS], ((0,), (0,))) + contract(
            phi_other, weights[2 * BLOCKS :], ((0,), (0,))
        )

    rotated_far = lax.ppermute(rotate(rotation_far), "band", Z_SWAP)

    gram = gram.reshape(4, BLOCKS, 4 * BLOCKS)
    place = (lax.axis_index("dom") >> 2) & 3
    pieces = [lax.dynamic_index_in_dim(gram, (place + k) & 3, 0, keepdims=False) for k in range(4)]
    for k in (2, 1, 3):
        pairs = [
            (chip(y, x, z), chip(y, (x + k) % 4, z)) for y in range(8) for x in range(4) for z in range(4)
        ]
        pieces[k] = lax.ppermute(pieces[k], "dom", pairs)
    terms, rotated_far = lax.optimization_barrier((pieces, rotated_far))
    terms = (terms[0] + terms[1]) + (terms[2] + terms[3])
    terms = terms.reshape(32, 4, 2, 2, BLOCKS).transpose(0, 3, 1, 2, 4).reshape(64, 8 * BLOCKS)
    terms = exchange(terms.reshape(64, 1, 8 * BLOCKS), PLANE_GROUPS)
    terms = jnp.sum(terms, axis=0)
    whole = lax.all_to_all(
        jnp.broadcast_to(terms[None], (BLOCKS, 1, 8 * BLOCKS)), "dom", 0, 0, tiled=True
    )
    whole = whole.reshape(8, 2, 2, 4, 4, 2, BLOCKS).transpose(5, 2, 1, 0, 3, 4, 6)
    whole = whole.reshape(2, 2, 2, BLOCKS, BLOCKS)
    whole = jnp.where(core == 0, whole, whole[:, :, ::-1])
    whole = whole.reshape(2, 4 * BLOCKS, BLOCKS)
    rotated_near = rotate(rotation_near)
    lower = jnp.where(z_hi == 0, rotated_near, rotated_far)
    upper = jnp.where(z_hi == 0, rotated_far, rotated_near)
    rotated = jnp.concatenate([lower, upper], axis=0).reshape(1, BX, BY, BZ, width)
    return (rotated, whole[0], whole[1])


def solution(mesh):
    in_specs = (
        P("dom", None, None, None, "band"),
        P("dom", None, None, None),
        P(),
        P(None, "band"),
    )
    out_specs = (P("dom", None, None, None, "band"), P(None, "band"), P(None, "band"))
    return jax.shard_map(local, mesh=mesh, in_specs=in_specs, out_specs=out_specs, check_vma=False)
```

```python
import jax
import jax.numpy as jnp
from jax import lax
from jax.experimental import pallas as pl
from jax.experimental.pallas import tpu as pltpu
from jax.sharding import PartitionSpec as P

STENCIL = (
    -5369.0 / 1800.0,
    12.0 / 7.0,
    -15.0 / 56.0,
    10.0 / 189.0,
    -1.0 / 112.0,
    2.0 / 1925.0,
    -1.0 / 16632.0,
)
REACH = 6
KINETIC = -0.5 / 0.36
BX, BY, BZ = 8, 12, 16
CELLS = BX * BY * BZ
HALF = CELLS // 2
PX, PY, PZ = 4, 4, 8
BLOCKS = PX * PY * PZ
LANES = 128
TILES = CELLS // LANES
HALF_TILES = HALF // LANES
SENT = TILES + HALF_TILES

ORDER = [(ix * PY + iy) * PZ + iz for iz in range(PZ) for iy in range(PY) for ix in range(PX)]
STEP_X, STEP_Y, STEP_Z = 1, PX, PX * PY


def flat(band, dom):
    return band * BLOCKS + dom


def chip(y, x, z):
    return (y * 4 + x) * 4 + z


CORE_GROUPS = [[flat(2 * h + c, d) for d in ORDER for h in range(2)] for c in range(2)]
PLANE_GROUPS = [
    [flat(2 * h + c, chip(y, x, z)) for y in range(8) for z in range(4) for h in range(2)]
    for c in range(2)
    for x in range(4)
]
CORE_SWAP = [(0, 1), (1, 0), (2, 3), (3, 2)]
Z_SWAP = [(0, 2), (2, 0), (1, 3), (3, 1)]
Z_MIRROR = [
    (flat(b, chip(y, x, z)), flat(b ^ 2, chip(y, x, 3 - z)))
    for b in range(4)
    for y in range(8)
    for x in range(4)
    for z in range(4)
]


def exchange(x, groups):
    return lax.all_to_all(x, ("band", "dom"), 0, 0, tiled=True, axis_index_groups=groups)


OX, OY, OZ = REACH, REACH, 8
EXT = (BX + 2 * REACH, BY + 2 * REACH, BZ + 16, LANES)


def pack_kernel(core_ref, orbitals_hbm, potential_hbm, out_ref, orbitals_ref, potential_ref, wide, sems):
    first = pltpu.make_async_copy(potential_hbm, potential_ref, sems.at[0])
    second = pltpu.make_async_copy(orbitals_hbm, orbitals_ref, sems.at[1])
    first.start()
    second.start()
    first.wait()
    wide[...] = jnp.concatenate([potential_ref[i] for i in range(BX)], axis=1)
    for s in range(HALF_TILES):
        row = wide[pl.ds(core_ref[0] * HALF_TILES + s, 1), :]
        out_ref[pl.ds(TILES + s, BLOCKS, stride=SENT), :] = jnp.broadcast_to(row, (BLOCKS, LANES))
    second.wait()
    for t in range(TILES):
        tile = orbitals_ref[t * LANES : (t + 1) * LANES]
        out_ref[pl.ds(t, BLOCKS, stride=SENT), :] = jnp.transpose(tile)


def packed(core, orbitals, potential):
    anywhere = pl.BlockSpec(memory_space=pl.ANY)
    return pl.pallas_call(
        pack_kernel,
        out_shape=jax.ShapeDtypeStruct((BLOCKS * SENT, LANES), jnp.float32),
        in_specs=[pl.BlockSpec(memory_space=pltpu.SMEM), anywhere, anywhere],
        out_specs=pl.BlockSpec(memory_space=pltpu.VMEM),
        scratch_shapes=[
            pltpu.VMEM((CELLS, LANES), jnp.float32),
            pltpu.VMEM((BX, BY, BZ), jnp.float32),
            pltpu.VMEM((BY, BX * BZ), jnp.float32),
            pltpu.SemaphoreType.DMA((2,)),
        ],
        compiler_params=pltpu.CompilerParams(vmem_limit_bytes=60 * 1024 * 1024),
    )(core, orbitals, potential)


def split_kernel(got_ref, phi_ref, both_ref):
    for m in range(2):
        for h in range(2):
            for t in range(HALF_TILES):
                tile = got_ref[pl.ds(h * TILES + m * HALF_TILES + t, BLOCKS, stride=2 * TILES), :]
                cells = slice(t * LANES, (t + 1) * LANES)
                at = (2 * m + h) * BLOCKS
                both_ref[at : at + BLOCKS, cells] = tile
                if m == 0:
                    phi_ref[at : at + BLOCKS, cells] = tile


def split_fields(got):
    vmem = pl.BlockSpec(memory_space=pltpu.VMEM)
    return pl.pallas_call(
        split_kernel,
        out_shape=(
            jax.ShapeDtypeStruct((2 * BLOCKS, HALF), jnp.float32),
            jax.ShapeDtypeStruct((4 * BLOCKS, HALF), jnp.float32),
        ),
        in_specs=[vmem],
        out_specs=(vmem, vmem),
        compiler_params=pltpu.CompilerParams(vmem_limit_bytes=16 * 1024 * 1024),
    )(got)


def margins(ext):
    lane = lax.broadcasted_iota(jnp.int32, (8, LANES), 1)
    iz, iy, ix = lane // STEP_Z, lane // STEP_Y % PY, lane // STEP_X % PX
    masks = {0: (ix > 0, ix < PX - 1), 1: (iy > 0, iy < PY - 1), 2: (iz > 0, iz < PZ - 1)}
    steps = (STEP_X, STEP_Y, STEP_Z)

    def carry(dim, to_below, to_above, from_below, from_above):
        below, above = masks[dim]
        ext[to_below] = jnp.where(below, pltpu.roll(ext[from_below], steps[dim], 1), 0.0)
        ext[to_above] = jnp.where(above, pltpu.roll(ext[from_above], LANES - steps[dim], 1), 0.0)

    def at(x, y, z):
        return (x, y, slice(z, z + 8))

    for x in range(OX, OX + BX):
        for y in range(OY, OY + BY):
            carry(2, at(x, y, OZ - 8), at(x, y, OZ + BZ), at(x, y, OZ + BZ - 8), at(x, y, OZ))
        for y in range(OY):
            for z in range(OZ, OZ + BZ, 8):
                carry(1, at(x, y, z), at(x, y + OY + BY, z), at(x, y + BY, z), at(x, y + OY, z))
    for x in range(OX):
        for y in range(OY, OY + BY):
            for z in range(OZ, OZ + BZ, 8):
                carry(0, at(x, y, z), at(x + OX + BX, y, z), at(x + BX, y, z), at(x + OX, y, z))


YS = BY // 2


def own(ext, i, y0):
    return ext[i + OX, OY + y0 : OY + y0 + YS, OZ : OZ + BZ]


def set_own(ext, i, y0, value):
    ext[i + OX, OY + y0 : OY + y0 + YS, OZ : OZ + BZ] = value


def laplace(ext, i, y0):
    at, y, z = i + OX, OY + y0, OZ
    total = (3.0 * STENCIL[0]) * ext[at, y : y + YS, z : z + BZ]
    for k in range(1, REACH + 1):
        pair_x = ext[at - k, y : y + YS, z : z + BZ] + ext[at + k, y : y + YS, z : z + BZ]
        pair_y = ext[at, y - k : y - k + YS, z : z + BZ] + ext[at, y + k : y + k + YS, z : z + BZ]
        pair_z = ext[at, y : y + YS, z - k : z - k + BZ] + ext[at, y : y + YS, z + k : z + k + BZ]
        total = total + STENCIL[k] * ((pair_x + pair_y) + pair_z)
    return total


def laplace_kernel(got_ref, x_ref, lap_ref, pot_ref, ext):
    for q in range(TILES):
        tile = jnp.transpose(got_ref[pl.ds(q, BLOCKS, stride=SENT), :]).reshape(LANES // BZ, BZ, LANES)
        for r in range(LANES // BZ):
            row = q * (LANES // BZ) + r
            ext[OX + row // BY, OY + row % BY, OZ : OZ + BZ] = tile[r]
            x_ref[row // BY, row % BY] = tile[r]
    for s in range(HALF_TILES):
        tile = jnp.transpose(got_ref[pl.ds(TILES + s, BLOCKS, stride=SENT), :])
        pot_ref[:, s] = tile.reshape(BX, BZ, LANES)
    margins(ext)

    def body(i, carry):
        for y0 in range(0, BY, YS):
            lap_ref[i, y0 : y0 + YS] = laplace(ext, i, y0)
        return carry

    lax.fori_loop(0, BX, body, 0)


def filter_coefficients(bounds_ref):
    lowest, cutoff, highest = (jnp.full((1, LANES), bounds_ref[k], jnp.float32) for k in range(3))
    half_width = (highest - cutoff) / 2.0
    centre = (highest + cutoff) / 2.0
    s1 = half_width / (lowest - centre)
    tau = 2.0 / s1
    s2 = 1.0 / (tau - s1)
    s3 = 1.0 / (tau - s2)
    scales = (s1 / half_width, 2.0 * s2 / half_width, 2.0 * s3 / half_width)
    return centre, scales, (None, s1 * s2, s2 * s3)


def filter_kernel(core_ref, bounds_ref, x_ref, lap_ref, pot_own_ref, v_other_ref, out_ref, ea, eb, pot, img):
    shift, scales, backs = filter_coefficients(bounds_ref)
    second = core_ref[0] == 1
    for s in range(HALF_TILES):
        other = jnp.transpose(v_other_ref[pl.ds(s, BLOCKS, stride=HALF_TILES), :]).reshape(BX, BZ, LANES)
        mine = pot_own_ref[:, s]
        pot[:, s] = jnp.where(second, other, mine)
        pot[:, s + HALF_TILES] = jnp.where(second, mine, other)

    def image(total, centre, i, y0):
        return KINETIC * total + (pot[i, y0 : y0 + YS] - shift) * centre

    def first(i, carry):
        for y0 in range(0, BY, YS):
            total, centre = lap_ref[i, y0 : y0 + YS], x_ref[i, y0 : y0 + YS]
            set_own(eb, i, y0, scales[0] * image(total, centre, i, y0))
        return carry

    def next_field(i, carry):
        for y0 in range(0, BY, YS):
            new = scales[1] * image(laplace(eb, i, y0), own(eb, i, y0), i, y0)
            set_own(ea, i, y0, new - backs[1] * x_ref[i, y0 : y0 + YS])
        return carry

    def last_field(i, squares):
        for y0 in range(0, BY, YS):
            new = scales[2] * image(laplace(ea, i, y0), own(ea, i, y0), i, y0)
            new = new - backs[2] * own(eb, i, y0)
            set_own(eb, i, y0, new)
            squares = squares + jnp.sum(new * new, axis=0)
        return squares

    def image_field(i, carry):
        for y0 in range(0, BY, YS):
            centre = own(eb, i, y0)
            img[i, y0 : y0 + YS] = KINETIC * laplace(eb, i, y0) + pot[i, y0 : y0 + YS] * centre
        return carry

    lax.fori_loop(0, BX, first, 0)
    margins(eb)
    lax.fori_loop(0, BX, next_field, 0)
    margins(ea)
    squares = lax.fori_loop(0, BX, last_field, jnp.zeros((BZ, LANES), jnp.float32))
    margins(eb)
    lax.fori_loop(0, BX, image_field, 0)
    norm = jnp.sqrt(jnp.sum(squares, keepdims=True))
    for q in range(TILES):
        rows = [q * (LANES // BZ) + r for r in range(LANES // BZ)]
        at = q // HALF_TILES * TILES + q % HALF_TILES
        field = jnp.concatenate([eb[OX + r // BY, OY + r % BY, OZ : OZ + BZ] for r in rows], 0)
        out_ref[pl.ds(at, BLOCKS, stride=2 * TILES), :] = jnp.transpose(field / norm)
        field = jnp.concatenate([img[r // BY, r % BY] for r in rows], 0)
        out_ref[pl.ds(at + HALF_TILES, BLOCKS, stride=2 * TILES), :] = jnp.transpose(field / norm)


FIELD = (BX, BY, BZ, LANES)


def first_laplace(got):
    vmem = pl.BlockSpec(memory_space=pltpu.VMEM)
    return pl.pallas_call(
        laplace_kernel,
        out_shape=(
            jax.ShapeDtypeStruct(FIELD, jnp.float32),
            jax.ShapeDtypeStruct(FIELD, jnp.float32),
            jax.ShapeDtypeStruct((BX, HALF_TILES, BZ, LANES), jnp.float32),
        ),
        in_specs=[vmem],
        out_specs=(vmem, vmem, vmem),
        scratch_shapes=[pltpu.VMEM(EXT, jnp.float32)],
        compiler_params=pltpu.CompilerParams(vmem_limit_bytes=24 * 1024 * 1024),
        cost_estimate=pl.CostEstimate(flops=20_000_000, bytes_accessed=20_000_000, transcendentals=0),
    )(got)


def filtered_fields(core, bounds, x, lap, pot_own, v_other):
    vmem = pl.BlockSpec(memory_space=pltpu.VMEM)
    return pl.pallas_call(
        filter_kernel,
        out_shape=jax.ShapeDtypeStruct((BLOCKS * 2 * TILES, LANES), jnp.float32),
        in_specs=[pl.BlockSpec(memory_space=pltpu.SMEM)] * 2 + [vmem] * 4,
        out_specs=vmem,
        scratch_shapes=[
            pltpu.VMEM(EXT, jnp.float32),
            pltpu.VMEM(EXT, jnp.float32),
            pltpu.VMEM(FIELD, jnp.float32),
            pltpu.VMEM(FIELD, jnp.float32),
        ],
        compiler_params=pltpu.CompilerParams(vmem_limit_bytes=36 * 1024 * 1024),
        cost_estimate=pl.CostEstimate(flops=60_000_000, bytes_accessed=40_000_000, transcendentals=0),
    )(core, bounds, x, lap, pot_own, v_other)


def contract(left, right, dims):
    return lax.dot_general(
        left,
        right,
        (dims, ((), ())),
        precision=lax.Precision.HIGH,
        preferred_element_type=jnp.float32,
    )


def local(orbitals, potential, bounds, rotation):
    width = rotation.shape[1]
    band = lax.axis_index("band")
    z_hi, core = band >> 1, band & 1
    here = core.reshape(1)

    sent = packed(here, orbitals.reshape(CELLS, width), potential[0])
    got = lax.all_to_all(
        sent.reshape(BLOCKS, 1, SENT * LANES), "dom", 0, 0, tiled=True, axis_index_groups=[ORDER]
    )
    got, rotation_near = lax.optimization_barrier((got, rotation))
    rotation_far = lax.ppermute(rotation_near, ("band", "dom"), Z_MIRROR)
    v_other = lax.ppermute(got[:, :, CELLS:], "band", CORE_SWAP)
    x, lap, pot_own = first_laplace(got.reshape(BLOCKS * SENT, LANES))
    images = filtered_fields(
        here, bounds, x, lap, pot_own, v_other.reshape(BLOCKS * HALF_TILES, LANES)
    )

    images, rotation_far = lax.optimization_barrier((images, rotation_far))
    got = exchange(images.reshape(2 * BLOCKS, 1, CELLS), CORE_GROUPS)
    got, rotation_near, rotation_far = lax.optimization_barrier((got, rotation_near, rotation_far))
    phi, both = split_fields(got.reshape(2 * BLOCKS * TILES, LANES))
    phi_other = lax.ppermute(phi, "band", CORE_SWAP)
    gram = jnp.concatenate(
        [contract(phi, both, ((1,), (1,))), contract(phi_other, both, ((1,), (1,)))], axis=0
    )

    def by_core(weights):
        weights = weights.reshape(2, 2, BLOCKS, width)
        swapped = jnp.where(core == 0, weights, weights[:, ::-1])
        return swapped.transpose(1, 0, 2, 3).reshape(4 * BLOCKS, width)

    def rotate(weights):
        return contract(phi, weights[: 2 * BLOCKS], ((0,), (0,))) + contract(
            phi_other, weights[2 * BLOCKS :], ((0,), (0,))
        )

    rotated_far = lax.ppermute(rotate(by_core(rotation_far)), "band", Z_SWAP)

    gram = gram.reshape(4, BLOCKS, 4 * BLOCKS)
    place = (lax.axis_index("dom") >> 2) & 3
    pieces = [lax.dynamic_index_in_dim(gram, (place + k) & 3, 0, keepdims=False) for k in range(4)]
    for k in (2, 1, 3):
        pairs = [
            (chip(y, x, z), chip(y, (x + k) % 4, z)) for y in range(8) for x in range(4) for z in range(4)
        ]
        pieces[k] = lax.ppermute(pieces[k], "dom", pairs)
    near = by_core(rotation_near)
    terms, rotated_far, near = lax.optimization_barrier((pieces, rotated_far, near))
    terms = (terms[0] + terms[1]) + (terms[2] + terms[3])
    terms = terms.reshape(32, 4, 2, 2, BLOCKS).transpose(0, 3, 1, 2, 4).reshape(64, 8 * BLOCKS)
    terms = exchange(terms.reshape(64, 1, 8 * BLOCKS), PLANE_GROUPS)
    rotated_near = rotate(near)
    lower = jnp.where(z_hi == 0, rotated_near, rotated_far)
    upper = jnp.where(z_hi == 0, rotated_far, rotated_near)
    rotated = jnp.concatenate([lower, upper], axis=0).reshape(1, BX, BY, BZ, width)
    terms, rotated = lax.optimization_barrier((terms, rotated))
    terms = jnp.sum(terms, axis=0)
    whole = lax.all_to_all(
        jnp.broadcast_to(terms[None], (BLOCKS, 1, 8 * BLOCKS)), "dom", 0, 0, tiled=True
    )
    whole = whole.reshape(8, 2, 2, 4, 4, 2, BLOCKS).transpose(5, 2, 1, 0, 3, 4, 6)
    whole = whole.reshape(2, 2, 2, BLOCKS, BLOCKS)
    whole = jnp.where(core == 0, whole, whole[:, :, ::-1])
    whole = whole.reshape(2, 4 * BLOCKS, BLOCKS)
    return (rotated, whole[0], whole[1])


def solution(mesh):
    in_specs = (
        P("dom", None, None, None, "band"),
        P("dom", None, None, None),
        P(),
        P(None, "band"),
    )
    out_specs = (P("dom", None, None, None, "band"), P(None, "band"), P(None, "band"))
    return jax.shard_map(local, mesh=mesh, in_specs=in_specs, out_specs=out_specs, check_vma=False)
```

```python
import jax
import jax.numpy as jnp
from jax import lax
from jax.experimental import pallas as pl
from jax.experimental.pallas import tpu as pltpu
from jax.sharding import PartitionSpec as P

STENCIL = (
    -5369.0 / 1800.0,
    12.0 / 7.0,
    -15.0 / 56.0,
    10.0 / 189.0,
    -1.0 / 112.0,
    2.0 / 1925.0,
    -1.0 / 16632.0,
)
REACH = 6
KINETIC = -0.5 / 0.36
BX, BY, BZ = 8, 12, 16
CELLS = BX * BY * BZ
HALF = CELLS // 2
PX, PY, PZ = 4, 4, 8
BLOCKS = PX * PY * PZ
LANES = 128
TILES = CELLS // LANES
HALF_TILES = HALF // LANES
SENT = TILES + HALF_TILES

ORDER = [(ix * PY + iy) * PZ + iz for iz in range(PZ) for iy in range(PY) for ix in range(PX)]
STEP_X, STEP_Y, STEP_Z = 1, PX, PX * PY


def flat(band, dom):
    return band * BLOCKS + dom


def chip(y, x, z):
    return (y * 4 + x) * 4 + z


CORE_GROUPS = [[flat(2 * h + c, d) for d in ORDER for h in range(2)] for c in range(2)]
PLANE_GROUPS = [
    [flat(2 * h + c, chip(y, x, z)) for y in range(8) for z in range(4) for h in range(2)]
    for c in range(2)
    for x in range(4)
]
CORE_SWAP = [(0, 1), (1, 0), (2, 3), (3, 2)]
Z_SWAP = [(0, 2), (2, 0), (1, 3), (3, 1)]
Z_MIRROR = [
    (flat(b, chip(y, x, z)), flat(b ^ 2, chip(y, x, 3 - z)))
    for b in range(4)
    for y in range(8)
    for x in range(4)
    for z in range(4)
]


def exchange(x, groups):
    return lax.all_to_all(x, ("band", "dom"), 0, 0, tiled=True, axis_index_groups=groups)


OX, OY, OZ = REACH, REACH, 8
EXT = (BX + 2 * REACH, BY + 2 * REACH, BZ + 16, LANES)


def pack_kernel(core_ref, orbitals_ref, potential_ref, out_ref, wide):
    for t in range(TILES):
        tile = orbitals_ref[t * LANES : (t + 1) * LANES]
        out_ref[pl.ds(t, BLOCKS, stride=SENT), :] = jnp.transpose(tile)
    wide[...] = jnp.concatenate([potential_ref[i] for i in range(BX)], axis=1)
    for s in range(HALF_TILES):
        row = wide[pl.ds(core_ref[0] * HALF_TILES + s, 1), :]
        out_ref[pl.ds(TILES + s, BLOCKS, stride=SENT), :] = jnp.broadcast_to(row, (BLOCKS, LANES))


def packed(core, orbitals, potential):
    vmem = pl.BlockSpec(memory_space=pltpu.VMEM)
    return pl.pallas_call(
        pack_kernel,
        out_shape=jax.ShapeDtypeStruct((BLOCKS * SENT, LANES), jnp.float32),
        in_specs=[pl.BlockSpec(memory_space=pltpu.SMEM), vmem, vmem],
        out_specs=vmem,
        scratch_shapes=[pltpu.VMEM((BY, BX * BZ), jnp.float32)],
        compiler_params=pltpu.CompilerParams(vmem_limit_bytes=16 * 1024 * 1024),
    )(core, orbitals, potential)


def split_kernel(got_ref, phi_ref, both_ref):
    for m in range(2):
        for h in range(2):
            for t in range(HALF_TILES):
                tile = got_ref[pl.ds(h * TILES + m * HALF_TILES + t, BLOCKS, stride=2 * TILES), :]
                cells = slice(t * LANES, (t + 1) * LANES)
                at = (2 * m + h) * BLOCKS
                both_ref[at : at + BLOCKS, cells] = tile
                if m == 0:
                    phi_ref[at : at + BLOCKS, cells] = tile


def split_fields(got):
    vmem = pl.BlockSpec(memory_space=pltpu.VMEM)
    return pl.pallas_call(
        split_kernel,
        out_shape=(
            jax.ShapeDtypeStruct((2 * BLOCKS, HALF), jnp.float32),
            jax.ShapeDtypeStruct((4 * BLOCKS, HALF), jnp.float32),
        ),
        in_specs=[vmem],
        out_specs=(vmem, vmem),
        compiler_params=pltpu.CompilerParams(vmem_limit_bytes=16 * 1024 * 1024),
    )(got)


def margins(ext):
    lane = lax.broadcasted_iota(jnp.int32, (8, LANES), 1)
    iz, iy, ix = lane // STEP_Z, lane // STEP_Y % PY, lane // STEP_X % PX
    masks = {0: (ix > 0, ix < PX - 1), 1: (iy > 0, iy < PY - 1), 2: (iz > 0, iz < PZ - 1)}
    steps = (STEP_X, STEP_Y, STEP_Z)

    def carry(dim, to_below, to_above, from_below, from_above):
        below, above = masks[dim]
        ext[to_below] = jnp.where(below, pltpu.roll(ext[from_below], steps[dim], 1), 0.0)
        ext[to_above] = jnp.where(above, pltpu.roll(ext[from_above], LANES - steps[dim], 1), 0.0)

    def at(x, y, z):
        return (x, y, slice(z, z + 8))

    for x in range(OX, OX + BX):
        for y in range(OY, OY + BY):
            carry(2, at(x, y, OZ - 8), at(x, y, OZ + BZ), at(x, y, OZ + BZ - 8), at(x, y, OZ))
        for y in range(OY):
            for z in range(OZ, OZ + BZ, 8):
                carry(1, at(x, y, z), at(x, y + OY + BY, z), at(x, y + BY, z), at(x, y + OY, z))
    for x in range(OX):
        for y in range(OY, OY + BY):
            for z in range(OZ, OZ + BZ, 8):
                carry(0, at(x, y, z), at(x + OX + BX, y, z), at(x + BX, y, z), at(x + OX, y, z))


YS = BY // 2


def own(ext, i, y0):
    return ext[i + OX, OY + y0 : OY + y0 + YS, OZ : OZ + BZ]


def set_own(ext, i, y0, value):
    ext[i + OX, OY + y0 : OY + y0 + YS, OZ : OZ + BZ] = value


def laplace(ext, i, y0):
    at, y, z = i + OX, OY + y0, OZ
    total = (3.0 * STENCIL[0]) * ext[at, y : y + YS, z : z + BZ]
    for k in range(1, REACH + 1):
        pair_x = ext[at - k, y : y + YS, z : z + BZ] + ext[at + k, y : y + YS, z : z + BZ]
        pair_y = ext[at, y - k : y - k + YS, z : z + BZ] + ext[at, y + k : y + k + YS, z : z + BZ]
        pair_z = ext[at, y : y + YS, z - k : z - k + BZ] + ext[at, y : y + YS, z + k : z + k + BZ]
        total = total + STENCIL[k] * ((pair_x + pair_y) + pair_z)
    return total


def laplace_kernel(got_ref, x_ref, lap_ref, pot_ref, ext):
    for q in range(TILES):
        tile = jnp.transpose(got_ref[pl.ds(q, BLOCKS, stride=SENT), :]).reshape(LANES // BZ, BZ, LANES)
        for r in range(LANES // BZ):
            row = q * (LANES // BZ) + r
            ext[OX + row // BY, OY + row % BY, OZ : OZ + BZ] = tile[r]
            x_ref[row // BY, row % BY] = tile[r]
    for s in range(HALF_TILES):
        tile = jnp.transpose(got_ref[pl.ds(TILES + s, BLOCKS, stride=SENT), :])
        pot_ref[:, s] = tile.reshape(BX, BZ, LANES)
    margins(ext)

    def body(i, carry):
        for y0 in range(0, BY, YS):
            lap_ref[i, y0 : y0 + YS] = laplace(ext, i, y0)
        return carry

    lax.fori_loop(0, BX, body, 0, unroll=True)


def filter_coefficients(bounds_ref):
    lowest, cutoff, highest = (jnp.full((1, LANES), bounds_ref[k], jnp.float32) for k in range(3))
    half_width = (highest - cutoff) / 2.0
    centre = (highest + cutoff) / 2.0
    s1 = half_width / (lowest - centre)
    tau = 2.0 / s1
    s2 = 1.0 / (tau - s1)
    s3 = 1.0 / (tau - s2)
    scales = (s1 / half_width, 2.0 * s2 / half_width, 2.0 * s3 / half_width)
    return centre, scales, (None, s1 * s2, s2 * s3)


def filter_kernel(core_ref, bounds_ref, x_ref, lap_ref, pot_own_ref, v_other_ref, out_ref, ea, eb, pot, img):
    shift, scales, backs = filter_coefficients(bounds_ref)
    second = core_ref[0] == 1
    for s in range(HALF_TILES):
        other = jnp.transpose(v_other_ref[pl.ds(s, BLOCKS, stride=HALF_TILES), :]).reshape(BX, BZ, LANES)
        mine = pot_own_ref[:, s]
        pot[:, s] = jnp.where(second, other, mine)
        pot[:, s + HALF_TILES] = jnp.where(second, mine, other)

    def image(total, centre, i, y0):
        return KINETIC * total + (pot[i, y0 : y0 + YS] - shift) * centre

    def first(i, carry):
        for y0 in range(0, BY, YS):
            total, centre = lap_ref[i, y0 : y0 + YS], x_ref[i, y0 : y0 + YS]
            set_own(eb, i, y0, scales[0] * image(total, centre, i, y0))
        return carry

    def next_field(i, carry):
        for y0 in range(0, BY, YS):
            new = scales[1] * image(laplace(eb, i, y0), own(eb, i, y0), i, y0)
            set_own(ea, i, y0, new - backs[1] * x_ref[i, y0 : y0 + YS])
        return carry

    def last_field(i, squares):
        for y0 in range(0, BY, YS):
            new = scales[2] * image(laplace(ea, i, y0), own(ea, i, y0), i, y0)
            new = new - backs[2] * own(eb, i, y0)
            set_own(eb, i, y0, new)
            squares = squares + jnp.sum(new * new, axis=0)
        return squares

    def image_field(i, carry):
        for y0 in range(0, BY, YS):
            centre = own(eb, i, y0)
            img[i, y0 : y0 + YS] = KINETIC * laplace(eb, i, y0) + pot[i, y0 : y0 + YS] * centre
        return carry

    lax.fori_loop(0, BX, first, 0, unroll=True)
    margins(eb)
    lax.fori_loop(0, BX, next_field, 0, unroll=True)
    margins(ea)
    squares = lax.fori_loop(0, BX, last_field, jnp.zeros((BZ, LANES), jnp.float32), unroll=True)
    margins(eb)
    lax.fori_loop(0, BX, image_field, 0, unroll=True)
    norm = jnp.sqrt(jnp.sum(squares, keepdims=True))
    for q in range(TILES):
        rows = [q * (LANES // BZ) + r for r in range(LANES // BZ)]
        at = q // HALF_TILES * TILES + q % HALF_TILES
        field = jnp.concatenate([eb[OX + r // BY, OY + r % BY, OZ : OZ + BZ] for r in rows], 0)
        out_ref[pl.ds(at, BLOCKS, stride=2 * TILES), :] = jnp.transpose(field / norm)
        field = jnp.concatenate([img[r // BY, r % BY] for r in rows], 0)
        out_ref[pl.ds(at + HALF_TILES, BLOCKS, stride=2 * TILES), :] = jnp.transpose(field / norm)


FIELD = (BX, BY, BZ, LANES)


def first_laplace(got):
    vmem = pl.BlockSpec(memory_space=pltpu.VMEM)
    return pl.pallas_call(
        laplace_kernel,
        out_shape=(
            jax.ShapeDtypeStruct(FIELD, jnp.float32),
            jax.ShapeDtypeStruct(FIELD, jnp.float32),
            jax.ShapeDtypeStruct((BX, HALF_TILES, BZ, LANES), jnp.float32),
        ),
        in_specs=[vmem],
        out_specs=(vmem, vmem, vmem),
        scratch_shapes=[pltpu.VMEM(EXT, jnp.float32)],
        compiler_params=pltpu.CompilerParams(vmem_limit_bytes=24 * 1024 * 1024),
        cost_estimate=pl.CostEstimate(flops=20_000_000, bytes_accessed=150_000_000, transcendentals=0),
    )(got)


def filtered_fields(core, bounds, x, lap, pot_own, v_other):
    vmem = pl.BlockSpec(memory_space=pltpu.VMEM)
    return pl.pallas_call(
        filter_kernel,
        out_shape=jax.ShapeDtypeStruct((BLOCKS * 2 * TILES, LANES), jnp.float32),
        in_specs=[pl.BlockSpec(memory_space=pltpu.SMEM)] * 2 + [vmem] * 4,
        out_specs=vmem,
        scratch_shapes=[
            pltpu.VMEM(EXT, jnp.float32),
            pltpu.VMEM(EXT, jnp.float32),
            pltpu.VMEM(FIELD, jnp.float32),
            pltpu.VMEM(FIELD, jnp.float32),
        ],
        compiler_params=pltpu.CompilerParams(vmem_limit_bytes=36 * 1024 * 1024),
        cost_estimate=pl.CostEstimate(flops=60_000_000, bytes_accessed=40_000_000, transcendentals=0),
    )(core, bounds, x, lap, pot_own, v_other)


def contract(left, right, dims):
    return lax.dot_general(
        left,
        right,
        (dims, ((), ())),
        precision=lax.Precision.HIGH,
        preferred_element_type=jnp.float32,
    )


def local(orbitals, potential, bounds, rotation):
    width = rotation.shape[1]
    band = lax.axis_index("band")
    z_hi, core = band >> 1, band & 1
    here = core.reshape(1)

    sent = packed(here, orbitals.reshape(CELLS, width), potential[0])
    got = lax.all_to_all(
        sent.reshape(BLOCKS, 1, SENT * LANES), "dom", 0, 0, tiled=True, axis_index_groups=[ORDER]
    )
    got, rotation_near = lax.optimization_barrier((got, rotation))
    rotation_far = lax.ppermute(rotation_near, ("band", "dom"), Z_MIRROR)
    v_other = lax.ppermute(got[:, :, CELLS:], "band", CORE_SWAP)
    x, lap, pot_own = first_laplace(got.reshape(BLOCKS * SENT, LANES))
    images = filtered_fields(
        here, bounds, x, lap, pot_own, v_other.reshape(BLOCKS * HALF_TILES, LANES)
    )

    spot = lax.axis_index("dom")
    images, rotation_far, spot, core, z_hi = lax.optimization_barrier(
        (images, rotation_far, spot, core, z_hi)
    )
    got = exchange(images.reshape(2 * BLOCKS, 1, CELLS), CORE_GROUPS)
    got, rotation_near, rotation_far, spot, core, z_hi = lax.optimization_barrier(
        (got, rotation_near, rotation_far, spot, core, z_hi)
    )
    phi, both = split_fields(got.reshape(2 * BLOCKS * TILES, LANES))
    phi_other = lax.ppermute(phi, "band", CORE_SWAP)
    gram = jnp.concatenate(
        [contract(phi, both, ((1,), (1,))), contract(phi_other, both, ((1,), (1,)))], axis=0
    )

    def by_core(weights):
        weights = weights.reshape(2, 2, BLOCKS, width)
        swapped = jnp.where(core == 0, weights, weights[:, ::-1])
        return swapped.transpose(1, 0, 2, 3).reshape(4 * BLOCKS, width)

    def rotate(weights):
        weights = by_core(weights)
        return contract(phi, weights[: 2 * BLOCKS], ((0,), (0,))) + contract(
            phi_other, weights[2 * BLOCKS :], ((0,), (0,))
        )

    rotated_far = lax.ppermute(rotate(rotation_far), "band", Z_SWAP)

    gram = gram.reshape(4, BLOCKS, 4 * BLOCKS)
    place = ((spot >> 2) & 3).astype(jnp.uint32)
    pieces = [lax.dynamic_index_in_dim(gram, place ^ k, 0, keepdims=False) for k in range(4)]
    for k in (2, 1, 3):
        pairs = [(chip(y, x, z), chip(y, x ^ k, z)) for y in range(8) for x in range(4) for z in range(4)]
        pieces[k] = lax.ppermute(pieces[k], "dom", pairs)
    terms, rotated_far = lax.optimization_barrier((pieces, rotated_far))
    terms = (terms[0] + terms[1]) + (terms[2] + terms[3])
    terms = terms.reshape(32, 4, 2, 2, BLOCKS).transpose(0, 3, 1, 2, 4).reshape(64, 8 * BLOCKS)
    terms = exchange(terms.reshape(64, 1, 8 * BLOCKS), PLANE_GROUPS)
    terms = jnp.sum(terms, axis=0)
    whole = lax.all_to_all(
        jnp.broadcast_to(terms[None], (BLOCKS, 1, 8 * BLOCKS)), "dom", 0, 0, tiled=True
    )
    whole = whole.reshape(8, 2, 2, 4, 4, 2, BLOCKS).transpose(5, 2, 1, 0, 3, 4, 6)
    whole = whole.reshape(2, 2, 2, BLOCKS, BLOCKS)
    whole = jnp.where(core == 0, whole, whole[:, :, ::-1])
    whole = whole.reshape(2, 4 * BLOCKS, BLOCKS)
    rotated_near = rotate(rotation_near)
    lower = jnp.where(z_hi == 0, rotated_near, rotated_far)
    upper = jnp.where(z_hi == 0, rotated_far, rotated_near)
    rotated = jnp.concatenate([lower, upper], axis=0).reshape(1, BX, BY, BZ, width)
    return (rotated, whole[0], whole[1])


def solution(mesh):
    in_specs = (
        P("dom", None, None, None, "band"),
        P("dom", None, None, None),
        P(),
        P(None, "band"),
    )
    out_specs = (P("dom", None, None, None, "band"), P(None, "band"), P(None, "band"))
    return jax.shard_map(local, mesh=mesh, in_specs=in_specs, out_specs=out_specs, check_vma=False)
```

```python
import jax
import jax.numpy as jnp
from jax import lax
from jax.experimental import pallas as pl
from jax.experimental.pallas import tpu as pltpu
from jax.sharding import PartitionSpec as P

STENCIL = (
    -5369.0 / 1800.0,
    12.0 / 7.0,
    -15.0 / 56.0,
    10.0 / 189.0,
    -1.0 / 112.0,
    2.0 / 1925.0,
    -1.0 / 16632.0,
)
REACH = 6
KINETIC = -0.5 / 0.36
BX, BY, BZ = 8, 12, 16
CELLS = BX * BY * BZ
HALF = CELLS // 2
PX, PY, PZ = 4, 4, 8
BLOCKS = PX * PY * PZ
LANES = 128
TILES = CELLS // LANES
HALF_TILES = HALF // LANES
SENT = TILES + HALF_TILES

ORDER = [(ix * PY + iy) * PZ + iz for iz in range(PZ) for iy in range(PY) for ix in range(PX)]
STEP_X, STEP_Y, STEP_Z = 1, PX, PX * PY


def flat(band, dom):
    return band * BLOCKS + dom


def chip(y, x, z):
    return (y * 4 + x) * 4 + z


CORE_GROUPS = [[flat(2 * h + c, d) for d in ORDER for h in range(2)] for c in range(2)]
PLANE_GROUPS = [
    [flat(2 * h + c, chip(y, x, z)) for y in range(8) for z in range(4) for h in range(2)]
    for c in range(2)
    for x in range(4)
]
CORE_SWAP = [(0, 1), (1, 0), (2, 3), (3, 2)]
Z_SWAP = [(0, 2), (2, 0), (1, 3), (3, 1)]
Z_MIRROR = [
    (flat(b, chip(y, x, z)), flat(b ^ 2, chip(y, x, 3 - z)))
    for b in range(4)
    for y in range(8)
    for x in range(4)
    for z in range(4)
]


def exchange(x, groups):
    return lax.all_to_all(x, ("band", "dom"), 0, 0, tiled=True, axis_index_groups=groups)


OX, OY, OZ = REACH, REACH, 8
EXT = (BX + 2 * REACH, BY + 2 * REACH, BZ + 16, LANES)


def pack_kernel(core_ref, orbitals_ref, potential_ref, out_ref, wide):
    for t in range(TILES):
        tile = orbitals_ref[t * LANES : (t + 1) * LANES]
        out_ref[pl.ds(t, BLOCKS, stride=SENT), :] = jnp.transpose(tile)
    wide[...] = jnp.concatenate([potential_ref[i] for i in range(BX)], axis=1)
    for s in range(HALF_TILES):
        row = wide[pl.ds(core_ref[0] * HALF_TILES + s, 1), :]
        out_ref[pl.ds(TILES + s, BLOCKS, stride=SENT), :] = jnp.broadcast_to(row, (BLOCKS, LANES))


def packed(core, orbitals, potential):
    vmem = pl.BlockSpec(memory_space=pltpu.VMEM)
    return pl.pallas_call(
        pack_kernel,
        out_shape=jax.ShapeDtypeStruct((BLOCKS * SENT, LANES), jnp.float32),
        in_specs=[pl.BlockSpec(memory_space=pltpu.SMEM), vmem, vmem],
        out_specs=vmem,
        scratch_shapes=[pltpu.VMEM((BY, BX * BZ), jnp.float32)],
        compiler_params=pltpu.CompilerParams(vmem_limit_bytes=16 * 1024 * 1024),
    )(core, orbitals, potential)


def split_kernel(got_ref, phi_ref, both_ref):
    for m in range(2):
        for h in range(2):
            for t in range(HALF_TILES):
                tile = got_ref[pl.ds(h * TILES + m * HALF_TILES + t, BLOCKS, stride=2 * TILES), :]
                cells = slice(t * LANES, (t + 1) * LANES)
                at = (2 * m + h) * BLOCKS
                both_ref[at : at + BLOCKS, cells] = tile
                if m == 0:
                    phi_ref[at : at + BLOCKS, cells] = tile


def split_fields(got):
    vmem = pl.BlockSpec(memory_space=pltpu.VMEM)
    return pl.pallas_call(
        split_kernel,
        out_shape=(
            jax.ShapeDtypeStruct((2 * BLOCKS, HALF), jnp.float32),
            jax.ShapeDtypeStruct((4 * BLOCKS, HALF), jnp.float32),
        ),
        in_specs=[vmem],
        out_specs=(vmem, vmem),
        compiler_params=pltpu.CompilerParams(vmem_limit_bytes=16 * 1024 * 1024),
    )(got)


def margins(ext):
    lane = lax.broadcasted_iota(jnp.int32, (8, LANES), 1)
    iz, iy, ix = lane // STEP_Z, lane // STEP_Y % PY, lane // STEP_X % PX
    masks = {0: (ix > 0, ix < PX - 1), 1: (iy > 0, iy < PY - 1), 2: (iz > 0, iz < PZ - 1)}
    steps = (STEP_X, STEP_Y, STEP_Z)

    def carry(dim, to_below, to_above, from_below, from_above):
        below, above = masks[dim]
        ext[to_below] = jnp.where(below, pltpu.roll(ext[from_below], steps[dim], 1), 0.0)
        ext[to_above] = jnp.where(above, pltpu.roll(ext[from_above], LANES - steps[dim], 1), 0.0)

    def at(x, y, z):
        return (x, y, slice(z, z + 8))

    for x in range(OX, OX + BX):
        for y in range(OY, OY + BY):
            carry(2, at(x, y, OZ - 8), at(x, y, OZ + BZ), at(x, y, OZ + BZ - 8), at(x, y, OZ))
        for y in range(OY):
            for z in range(OZ, OZ + BZ, 8):
                carry(1, at(x, y, z), at(x, y + OY + BY, z), at(x, y + BY, z), at(x, y + OY, z))
    for x in range(OX):
        for y in range(OY, OY + BY):
            for z in range(OZ, OZ + BZ, 8):
                carry(0, at(x, y, z), at(x + OX + BX, y, z), at(x + BX, y, z), at(x + OX, y, z))


YS = BY // 2


def own(ext, i, y0):
    return ext[i + OX, OY + y0 : OY + y0 + YS, OZ : OZ + BZ]


def set_own(ext, i, y0, value):
    ext[i + OX, OY + y0 : OY + y0 + YS, OZ : OZ + BZ] = value


def laplace(ext, i, y0):
    at, y, z = i + OX, OY + y0, OZ
    total = (3.0 * STENCIL[0]) * ext[at, y : y + YS, z : z + BZ]
    for k in range(1, REACH + 1):
        pair_x = ext[at - k, y : y + YS, z : z + BZ] + ext[at + k, y : y + YS, z : z + BZ]
        pair_y = ext[at, y - k : y - k + YS, z : z + BZ] + ext[at, y + k : y + k + YS, z : z + BZ]
        pair_z = ext[at, y : y + YS, z - k : z - k + BZ] + ext[at, y : y + YS, z + k : z + k + BZ]
        total = total + STENCIL[k] * ((pair_x + pair_y) + pair_z)
    return total


def laplace_kernel(got_ref, x_ref, lap_ref, pot_ref, ext):
    for q in range(TILES):
        tile = jnp.transpose(got_ref[pl.ds(q, BLOCKS, stride=SENT), :]).reshape(LANES // BZ, BZ, LANES)
        for r in range(LANES // BZ):
            row = q * (LANES // BZ) + r
            ext[OX + row // BY, OY + row % BY, OZ : OZ + BZ] = tile[r]
            x_ref[row // BY, row % BY] = tile[r]
    for s in range(HALF_TILES):
        tile = jnp.transpose(got_ref[pl.ds(TILES + s, BLOCKS, stride=SENT), :])
        pot_ref[:, s] = tile.reshape(BX, BZ, LANES)
    margins(ext)

    def body(i, carry):
        for y0 in range(0, BY, YS):
            lap_ref[i, y0 : y0 + YS] = laplace(ext, i, y0)
        return carry

    lax.fori_loop(0, BX, body, 0, unroll=True)


def filter_coefficients(bounds_ref):
    lowest, cutoff, highest = (jnp.full((1, LANES), bounds_ref[k], jnp.float32) for k in range(3))
    half_width = (highest - cutoff) / 2.0
    centre = (highest + cutoff) / 2.0
    s1 = half_width / (lowest - centre)
    tau = 2.0 / s1
    s2 = 1.0 / (tau - s1)
    s3 = 1.0 / (tau - s2)
    scales = (s1 / half_width, 2.0 * s2 / half_width, 2.0 * s3 / half_width)
    return centre, scales, (None, s1 * s2, s2 * s3)


def filter_kernel(core_ref, bounds_ref, x_ref, lap_ref, pot_own_ref, v_other_ref, out_ref, ea, eb, pot, img):
    shift, scales, backs = filter_coefficients(bounds_ref)
    second = core_ref[0] == 1
    for s in range(HALF_TILES):
        other = jnp.transpose(v_other_ref[pl.ds(s, BLOCKS, stride=HALF_TILES), :]).reshape(BX, BZ, LANES)
        mine = pot_own_ref[:, s]
        pot[:, s] = jnp.where(second, other, mine)
        pot[:, s + HALF_TILES] = jnp.where(second, mine, other)

    def image(total, centre, i, y0):
        return KINETIC * total + (pot[i, y0 : y0 + YS] - shift) * centre

    def first(i, carry):
        for y0 in range(0, BY, YS):
            total, centre = lap_ref[i, y0 : y0 + YS], x_ref[i, y0 : y0 + YS]
            set_own(eb, i, y0, scales[0] * image(total, centre, i, y0))
        return carry

    def next_field(i, carry):
        for y0 in range(0, BY, YS):
            new = scales[1] * image(laplace(eb, i, y0), own(eb, i, y0), i, y0)
            set_own(ea, i, y0, new - backs[1] * x_ref[i, y0 : y0 + YS])
        return carry

    def last_field(i, squares):
        for y0 in range(0, BY, YS):
            new = scales[2] * image(laplace(ea, i, y0), own(ea, i, y0), i, y0)
            new = new - backs[2] * own(eb, i, y0)
            set_own(eb, i, y0, new)
            squares = squares + jnp.sum(new * new, axis=0)
        return squares

    def image_field(i, carry):
        for y0 in range(0, BY, YS):
            centre = own(eb, i, y0)
            img[i, y0 : y0 + YS] = KINETIC * laplace(eb, i, y0) + pot[i, y0 : y0 + YS] * centre
        return carry

    lax.fori_loop(0, BX, first, 0, unroll=True)
    margins(eb)
    lax.fori_loop(0, BX, next_field, 0, unroll=True)
    margins(ea)
    squares = lax.fori_loop(0, BX, last_field, jnp.zeros((BZ, LANES), jnp.float32), unroll=True)
    margins(eb)
    lax.fori_loop(0, BX, image_field, 0, unroll=True)
    norm = jnp.sqrt(jnp.sum(squares, keepdims=True))
    for q in range(TILES):
        rows = [q * (LANES // BZ) + r for r in range(LANES // BZ)]
        at = q // HALF_TILES * TILES + q % HALF_TILES
        field = jnp.concatenate([eb[OX + r // BY, OY + r % BY, OZ : OZ + BZ] for r in rows], 0)
        out_ref[pl.ds(at, BLOCKS, stride=2 * TILES), :] = jnp.transpose(field / norm)
        field = jnp.concatenate([img[r // BY, r % BY] for r in rows], 0)
        out_ref[pl.ds(at + HALF_TILES, BLOCKS, stride=2 * TILES), :] = jnp.transpose(field / norm)


FIELD = (BX, BY, BZ, LANES)


def first_laplace(got):
    vmem = pl.BlockSpec(memory_space=pltpu.VMEM)
    return pl.pallas_call(
        laplace_kernel,
        out_shape=(
            jax.ShapeDtypeStruct(FIELD, jnp.float32),
            jax.ShapeDtypeStruct(FIELD, jnp.float32),
            jax.ShapeDtypeStruct((BX, HALF_TILES, BZ, LANES), jnp.float32),
        ),
        in_specs=[vmem],
        out_specs=(vmem, vmem, vmem),
        scratch_shapes=[pltpu.VMEM(EXT, jnp.float32)],
        compiler_params=pltpu.CompilerParams(vmem_limit_bytes=24 * 1024 * 1024),
        cost_estimate=pl.CostEstimate(flops=20_000_000, bytes_accessed=150_000_000, transcendentals=0),
    )(got)


def filtered_fields(core, bounds, x, lap, pot_own, v_other):
    vmem = pl.BlockSpec(memory_space=pltpu.VMEM)
    return pl.pallas_call(
        filter_kernel,
        out_shape=jax.ShapeDtypeStruct((BLOCKS * 2 * TILES, LANES), jnp.float32),
        in_specs=[pl.BlockSpec(memory_space=pltpu.SMEM)] * 2 + [vmem] * 4,
        out_specs=vmem,
        scratch_shapes=[
            pltpu.VMEM(EXT, jnp.float32),
            pltpu.VMEM(EXT, jnp.float32),
            pltpu.VMEM(FIELD, jnp.float32),
            pltpu.VMEM(FIELD, jnp.float32),
        ],
        compiler_params=pltpu.CompilerParams(vmem_limit_bytes=36 * 1024 * 1024),
        cost_estimate=pl.CostEstimate(flops=60_000_000, bytes_accessed=40_000_000, transcendentals=0),
    )(core, bounds, x, lap, pot_own, v_other)


def contract(left, right, dims):
    return lax.dot_general(
        left,
        right,
        (dims, ((), ())),
        precision=lax.Precision.HIGH,
        preferred_element_type=jnp.float32,
    )


def local(orbitals, potential, bounds, rotation):
    width = rotation.shape[1]
    band = lax.axis_index("band")
    z_hi, core = band >> 1, band & 1
    here = core.reshape(1)

    sent = packed(here, orbitals.reshape(CELLS, width), potential[0])
    got = lax.all_to_all(
        sent.reshape(BLOCKS, 1, SENT * LANES), "dom", 0, 0, tiled=True, axis_index_groups=[ORDER]
    )
    rotation_far = lax.ppermute(rotation, ("band", "dom"), Z_MIRROR)
    got, rotation_far = lax.optimization_barrier((got, rotation_far))
    v_other = lax.ppermute(got[:, :, CELLS:], "band", CORE_SWAP)
    x, lap, pot_own = first_laplace(got.reshape(BLOCKS * SENT, LANES))
    images = filtered_fields(
        here, bounds, x, lap, pot_own, v_other.reshape(BLOCKS * HALF_TILES, LANES)
    )

    spot = lax.axis_index("dom")
    got = exchange(images.reshape(2 * BLOCKS, 1, CELLS), CORE_GROUPS)
    got, rotation_near, rotation_far = lax.optimization_barrier((got, rotation, rotation_far))
    phi, both = split_fields(got.reshape(2 * BLOCKS * TILES, LANES))
    phi_other = lax.ppermute(phi, "band", CORE_SWAP)
    gram = jnp.concatenate(
        [contract(phi, both, ((1,), (1,))), contract(phi_other, both, ((1,), (1,)))], axis=0
    )

    def by_core(weights):
        weights = weights.reshape(2, 2, BLOCKS, width)
        swapped = jnp.where(core == 0, weights, weights[:, ::-1])
        return swapped.transpose(1, 0, 2, 3).reshape(4 * BLOCKS, width)

    def rotate(weights):
        weights = by_core(weights)
        return contract(phi, weights[: 2 * BLOCKS], ((0,), (0,))) + contract(
            phi_other, weights[2 * BLOCKS :], ((0,), (0,))
        )

    rotated_far = lax.ppermute(rotate(rotation_far), "band", Z_SWAP)

    gram = gram.reshape(4, BLOCKS, 4 * BLOCKS)
    place = ((spot >> 2) & 3).astype(jnp.uint32)
    pieces = [lax.dynamic_index_in_dim(gram, (place + k) & 3, 0, keepdims=False) for k in range(4)]
    for k in (2, 1, 3):
        pairs = [
            (chip(y, x, z), chip(y, (x + k) % 4, z)) for y in range(8) for x in range(4) for z in range(4)
        ]
        pieces[k] = lax.ppermute(pieces[k], "dom", pairs)
    terms, rotated_far = lax.optimization_barrier((pieces, rotated_far))
    terms = (terms[0] + terms[1]) + (terms[2] + terms[3])
    terms = terms.reshape(32, 4, 2, 2, BLOCKS).transpose(0, 3, 1, 2, 4).reshape(64, 8 * BLOCKS)
    terms = exchange(terms.reshape(64, 1, 8 * BLOCKS), PLANE_GROUPS)
    terms = jnp.sum(terms, axis=0)
    whole = lax.all_to_all(
        jnp.broadcast_to(terms[None], (BLOCKS, 1, 8 * BLOCKS)), "dom", 0, 0, tiled=True
    )
    whole = whole.reshape(8, 2, 2, 4, 4, 2, BLOCKS).transpose(5, 2, 1, 0, 3, 4, 6)
    whole = whole.reshape(2, 2, 2, BLOCKS, BLOCKS)
    whole = jnp.where(core == 0, whole, whole[:, :, ::-1])
    whole = whole.reshape(2, 4 * BLOCKS, BLOCKS)
    rotated_near = rotate(rotation_near)
    lower = jnp.where(z_hi == 0, rotated_near, rotated_far)
    upper = jnp.where(z_hi == 0, rotated_far, rotated_near)
    rotated = jnp.concatenate([lower, upper], axis=0).reshape(1, BX, BY, BZ, width)
    return (rotated, whole[0], whole[1])


def solution(mesh):
    in_specs = (
        P("dom", None, None, None, "band"),
        P("dom", None, None, None),
        P(),
        P(None, "band"),
    )
    out_specs = (P("dom", None, None, None, "band"), P(None, "band"), P(None, "band"))
    return jax.shard_map(local, mesh=mesh, in_specs=in_specs, out_specs=out_specs, check_vma=False)
```

```python
import jax
import jax.numpy as jnp
from jax import lax
from jax.experimental import pallas as pl
from jax.experimental.pallas import tpu as pltpu
from jax.sharding import PartitionSpec as P

STENCIL = (
    -5369.0 / 1800.0,
    12.0 / 7.0,
    -15.0 / 56.0,
    10.0 / 189.0,
    -1.0 / 112.0,
    2.0 / 1925.0,
    -1.0 / 16632.0,
)
REACH = 6
KINETIC = -0.5 / 0.36
BX, BY, BZ = 8, 12, 16
CELLS = BX * BY * BZ
HALF = CELLS // 2
PX, PY, PZ = 4, 4, 8
BLOCKS = PX * PY * PZ
LANES = 128
TILES = CELLS // LANES
HALF_TILES = HALF // LANES
SENT = TILES + HALF_TILES

ORDER = [(ix * PY + iy) * PZ + iz for iz in range(PZ) for iy in range(PY) for ix in range(PX)]
STEP_X, STEP_Y, STEP_Z = 1, PX, PX * PY


def flat(band, dom):
    return band * BLOCKS + dom


def chip(y, x, z):
    return (y * 4 + x) * 4 + z


CORE_GROUPS = [[flat(2 * h + c, d) for d in ORDER for h in range(2)] for c in range(2)]
PLANE_GROUPS = [
    [flat(2 * h + c, chip(y, x, z)) for y in range(8) for z in range(4) for h in range(2)]
    for c in range(2)
    for x in range(4)
]
CORE_SWAP = [(0, 1), (1, 0), (2, 3), (3, 2)]
Z_SWAP = [(0, 2), (2, 0), (1, 3), (3, 1)]
Z_MIRROR = [
    (flat(b, chip(y, x, z)), flat(b ^ 2, chip(y, x, 3 - z)))
    for b in range(4)
    for y in range(8)
    for x in range(4)
    for z in range(4)
]


def exchange(x, groups):
    return lax.all_to_all(x, ("band", "dom"), 0, 0, tiled=True, axis_index_groups=groups)


OX, OY, OZ = REACH, REACH, 8
EXT = (BX + 2 * REACH, BY + 2 * REACH, BZ + 16, LANES)


def pack_kernel(core_ref, orbitals_ref, potential_ref, out_ref):
    for t in range(TILES):
        tile = orbitals_ref[t * LANES : (t + 1) * LANES]
        out_ref[pl.ds(t, BLOCKS, stride=SENT), :] = jnp.transpose(tile)
    for s in range(HALF_TILES):
        plane = potential_ref[core_ref[0] * HALF_TILES + s]
        row = jnp.concatenate([plane[i : i + 1] for i in range(BX)], axis=1)
        out_ref[pl.ds(TILES + s, BLOCKS, stride=SENT), :] = jnp.broadcast_to(row, (BLOCKS, LANES))


def packed(core, orbitals, potential):
    vmem = pl.BlockSpec(memory_space=pltpu.VMEM)
    return pl.pallas_call(
        pack_kernel,
        out_shape=jax.ShapeDtypeStruct((BLOCKS * SENT, LANES), jnp.float32),
        in_specs=[pl.BlockSpec(memory_space=pltpu.SMEM), vmem, vmem],
        out_specs=vmem,
        compiler_params=pltpu.CompilerParams(vmem_limit_bytes=16 * 1024 * 1024),
    )(core, orbitals, potential)


def split_kernel(got_ref, phi_ref, both_ref):
    for m in range(2):
        for h in range(2):
            for t in range(HALF_TILES):
                tile = got_ref[pl.ds(h * TILES + m * HALF_TILES + t, BLOCKS, stride=2 * TILES), :]
                cells = slice(t * LANES, (t + 1) * LANES)
                at = (2 * m + h) * BLOCKS
                both_ref[at : at + BLOCKS, cells] = tile
                if m == 0:
                    phi_ref[at : at + BLOCKS, cells] = tile


def split_fields(got):
    vmem = pl.BlockSpec(memory_space=pltpu.VMEM)
    return pl.pallas_call(
        split_kernel,
        out_shape=(
            jax.ShapeDtypeStruct((2 * BLOCKS, HALF), jnp.float32),
            jax.ShapeDtypeStruct((4 * BLOCKS, HALF), jnp.float32),
        ),
        in_specs=[vmem],
        out_specs=(vmem, vmem),
        compiler_params=pltpu.CompilerParams(vmem_limit_bytes=16 * 1024 * 1024),
    )(got)


def margins(ext):
    lane = lax.broadcasted_iota(jnp.int32, (8, LANES), 1)
    iz, iy, ix = lane // STEP_Z, lane // STEP_Y % PY, lane // STEP_X % PX
    masks = {0: (ix > 0, ix < PX - 1), 1: (iy > 0, iy < PY - 1), 2: (iz > 0, iz < PZ - 1)}
    steps = (STEP_X, STEP_Y, STEP_Z)

    def carry(dim, to_below, to_above, from_below, from_above):
        below, above = masks[dim]
        ext[to_below] = jnp.where(below, pltpu.roll(ext[from_below], steps[dim], 1), 0.0)
        ext[to_above] = jnp.where(above, pltpu.roll(ext[from_above], LANES - steps[dim], 1), 0.0)

    def at(x, y, z):
        return (x, y, slice(z, z + 8))

    for x in range(OX, OX + BX):
        for y in range(OY, OY + BY):
            carry(2, at(x, y, OZ - 8), at(x, y, OZ + BZ), at(x, y, OZ + BZ - 8), at(x, y, OZ))
        for y in range(OY):
            for z in range(OZ, OZ + BZ, 8):
                carry(1, at(x, y, z), at(x, y + OY + BY, z), at(x, y + BY, z), at(x, y + OY, z))
    for x in range(OX):
        for y in range(OY, OY + BY):
            for z in range(OZ, OZ + BZ, 8):
                carry(0, at(x, y, z), at(x + OX + BX, y, z), at(x + BX, y, z), at(x + OX, y, z))


YS = BY // 2


def own(ext, i, y0):
    return ext[i + OX, OY + y0 : OY + y0 + YS, OZ : OZ + BZ]


def set_own(ext, i, y0, value):
    ext[i + OX, OY + y0 : OY + y0 + YS, OZ : OZ + BZ] = value


def laplace(ext, i, y0):
    at, y, z = i + OX, OY + y0, OZ
    total = (3.0 * STENCIL[0]) * ext[at, y : y + YS, z : z + BZ]
    for k in range(1, REACH + 1):
        pair_x = ext[at - k, y : y + YS, z : z + BZ] + ext[at + k, y : y + YS, z : z + BZ]
        pair_y = ext[at, y - k : y - k + YS, z : z + BZ] + ext[at, y + k : y + k + YS, z : z + BZ]
        pair_z = ext[at, y : y + YS, z - k : z - k + BZ] + ext[at, y : y + YS, z + k : z + k + BZ]
        total = total + STENCIL[k] * ((pair_x + pair_y) + pair_z)
    return total


def laplace_kernel(got_ref, x_ref, lap_ref, pot_ref, ext):
    for q in range(TILES):
        tile = jnp.transpose(got_ref[pl.ds(q, BLOCKS, stride=SENT), :]).reshape(LANES // BZ, BZ, LANES)
        for r in range(LANES // BZ):
            row = q * (LANES // BZ) + r
            ext[OX + row // BY, OY + row % BY, OZ : OZ + BZ] = tile[r]
            x_ref[row // BY, row % BY] = tile[r]
    for s in range(HALF_TILES):
        tile = jnp.transpose(got_ref[pl.ds(TILES + s, BLOCKS, stride=SENT), :])
        pot_ref[:, s] = tile.reshape(BX, BZ, LANES)
    margins(ext)

    def body(i, carry):
        for y0 in range(0, BY, YS):
            lap_ref[i, y0 : y0 + YS] = laplace(ext, i, y0)
        return carry

    lax.fori_loop(0, BX, body, 0, unroll=True)


def filter_coefficients(bounds_ref):
    lowest, cutoff, highest = (jnp.full((1, LANES), bounds_ref[k], jnp.float32) for k in range(3))
    half_width = (highest - cutoff) / 2.0
    centre = (highest + cutoff) / 2.0
    s1 = half_width / (lowest - centre)
    tau = 2.0 / s1
    s2 = 1.0 / (tau - s1)
    s3 = 1.0 / (tau - s2)
    scales = (s1 / half_width, 2.0 * s2 / half_width, 2.0 * s3 / half_width)
    return centre, scales, (None, s1 * s2, s2 * s3)


def filter_kernel(core_ref, bounds_ref, x_ref, lap_ref, pot_own_ref, v_other_ref, out_ref, ea, eb, pot, img):
    shift, scales, backs = filter_coefficients(bounds_ref)
    second = core_ref[0] == 1
    for s in range(HALF_TILES):
        other = jnp.transpose(v_other_ref[pl.ds(s, BLOCKS, stride=HALF_TILES), :]).reshape(BX, BZ, LANES)
        mine = pot_own_ref[:, s]
        pot[:, s] = jnp.where(second, other, mine)
        pot[:, s + HALF_TILES] = jnp.where(second, mine, other)

    def image(total, centre, i, y0):
        return KINETIC * total + (pot[i, y0 : y0 + YS] - shift) * centre

    def first(i, carry):
        for y0 in range(0, BY, YS):
            total, centre = lap_ref[i, y0 : y0 + YS], x_ref[i, y0 : y0 + YS]
            set_own(eb, i, y0, scales[0] * image(total, centre, i, y0))
        return carry

    def next_field(i, carry):
        for y0 in range(0, BY, YS):
            new = scales[1] * image(laplace(eb, i, y0), own(eb, i, y0), i, y0)
            set_own(ea, i, y0, new - backs[1] * x_ref[i, y0 : y0 + YS])
        return carry

    def last_field(i, squares):
        for y0 in range(0, BY, YS):
            new = scales[2] * image(laplace(ea, i, y0), own(ea, i, y0), i, y0)
            new = new - backs[2] * own(eb, i, y0)
            set_own(eb, i, y0, new)
            squares = squares + jnp.sum(new * new, axis=0)
        return squares

    def image_field(i, carry):
        for y0 in range(0, BY, YS):
            centre = own(eb, i, y0)
            img[i, y0 : y0 + YS] = KINETIC * laplace(eb, i, y0) + pot[i, y0 : y0 + YS] * centre
        return carry

    lax.fori_loop(0, BX, first, 0, unroll=True)
    margins(eb)
    lax.fori_loop(0, BX, next_field, 0, unroll=True)
    margins(ea)
    squares = lax.fori_loop(0, BX, last_field, jnp.zeros((BZ, LANES), jnp.float32), unroll=True)
    margins(eb)
    lax.fori_loop(0, BX, image_field, 0, unroll=True)
    norm = jnp.sqrt(jnp.sum(squares, keepdims=True))
    for q in range(TILES):
        rows = [q * (LANES // BZ) + r for r in range(LANES // BZ)]
        at = q // HALF_TILES * TILES + q % HALF_TILES
        field = jnp.concatenate([eb[OX + r // BY, OY + r % BY, OZ : OZ + BZ] for r in rows], 0)
        out_ref[pl.ds(at, BLOCKS, stride=2 * TILES), :] = jnp.transpose(field / norm)
        field = jnp.concatenate([img[r // BY, r % BY] for r in rows], 0)
        out_ref[pl.ds(at + HALF_TILES, BLOCKS, stride=2 * TILES), :] = jnp.transpose(field / norm)


FIELD = (BX, BY, BZ, LANES)


def first_laplace(got):
    vmem = pl.BlockSpec(memory_space=pltpu.VMEM)
    return pl.pallas_call(
        laplace_kernel,
        out_shape=(
            jax.ShapeDtypeStruct(FIELD, jnp.float32),
            jax.ShapeDtypeStruct(FIELD, jnp.float32),
            jax.ShapeDtypeStruct((BX, HALF_TILES, BZ, LANES), jnp.float32),
        ),
        in_specs=[vmem],
        out_specs=(vmem, vmem, vmem),
        scratch_shapes=[pltpu.VMEM(EXT, jnp.float32)],
        compiler_params=pltpu.CompilerParams(vmem_limit_bytes=24 * 1024 * 1024),
        cost_estimate=pl.CostEstimate(flops=20_000_000, bytes_accessed=150_000_000, transcendentals=0),
    )(got)


def filtered_fields(core, bounds, x, lap, pot_own, v_other):
    vmem = pl.BlockSpec(memory_space=pltpu.VMEM)
    return pl.pallas_call(
        filter_kernel,
        out_shape=jax.ShapeDtypeStruct((BLOCKS * 2 * TILES, LANES), jnp.float32),
        in_specs=[pl.BlockSpec(memory_space=pltpu.SMEM)] * 2 + [vmem] * 4,
        out_specs=vmem,
        scratch_shapes=[
            pltpu.VMEM(EXT, jnp.float32),
            pltpu.VMEM(EXT, jnp.float32),
            pltpu.VMEM(FIELD, jnp.float32),
            pltpu.VMEM(FIELD, jnp.float32),
        ],
        compiler_params=pltpu.CompilerParams(vmem_limit_bytes=36 * 1024 * 1024),
        cost_estimate=pl.CostEstimate(flops=60_000_000, bytes_accessed=40_000_000, transcendentals=0),
    )(core, bounds, x, lap, pot_own, v_other)


def contract(left, right, dims):
    return lax.dot_general(
        left,
        right,
        (dims, ((), ())),
        precision=lax.Precision.HIGH,
        preferred_element_type=jnp.float32,
    )


def local(orbitals, potential, bounds, rotation):
    width = rotation.shape[1]
    band = lax.axis_index("band")
    z_hi, core = band >> 1, band & 1
    here = core.reshape(1)

    sent = packed(here, orbitals.reshape(CELLS, width), potential[0].transpose(1, 0, 2))
    got = lax.all_to_all(
        sent.reshape(BLOCKS, 1, SENT * LANES), "dom", 0, 0, tiled=True, axis_index_groups=[ORDER]
    )
    rotation_far = lax.ppermute(rotation, ("band", "dom"), Z_MIRROR)
    got, rotation_far = lax.optimization_barrier((got, rotation_far))
    v_other = lax.ppermute(got[:, :, CELLS:], "band", CORE_SWAP)
    x, lap, pot_own = first_laplace(got.reshape(BLOCKS * SENT, LANES))
    images = filtered_fields(
        here, bounds, x, lap, pot_own, v_other.reshape(BLOCKS * HALF_TILES, LANES)
    )

    spot = lax.axis_index("dom")
    got = exchange(images.reshape(2 * BLOCKS, 1, CELLS), CORE_GROUPS)
    got, rotation_near, rotation_far = lax.optimization_barrier((got, rotation, rotation_far))
    phi, both = split_fields(got.reshape(2 * BLOCKS * TILES, LANES))
    phi_other = lax.ppermute(phi, "band", CORE_SWAP)
    gram = jnp.concatenate(
        [contract(phi, both, ((1,), (1,))), contract(phi_other, both, ((1,), (1,)))], axis=0
    )

    def by_core(weights):
        weights = weights.reshape(2, 2, BLOCKS, width)
        swapped = jnp.where(core == 0, weights, weights[:, ::-1])
        return swapped.transpose(1, 0, 2, 3).reshape(4 * BLOCKS, width)

    def rotate(weights):
        weights = by_core(weights)
        return contract(phi, weights[: 2 * BLOCKS], ((0,), (0,))) + contract(
            phi_other, weights[2 * BLOCKS :], ((0,), (0,))
        )

    rotated_far = lax.ppermute(rotate(rotation_far), "band", Z_SWAP)

    gram = gram.reshape(4, BLOCKS, 4 * BLOCKS)
    place = ((spot >> 2) & 3).astype(jnp.uint32)
    pieces = [lax.dynamic_index_in_dim(gram, (place + k) & 3, 0, keepdims=False) for k in range(4)]
    for k in (2, 1, 3):
        pairs = [
            (chip(y, x, z), chip(y, (x + k) % 4, z)) for y in range(8) for x in range(4) for z in range(4)
        ]
        pieces[k] = lax.ppermute(pieces[k], "dom", pairs)
    terms, rotated_far = lax.optimization_barrier((pieces, rotated_far))
    terms = (terms[0] + terms[1]) + (terms[2] + terms[3])
    terms = terms.reshape(32, 4, 2, 2, BLOCKS).transpose(0, 3, 1, 2, 4).reshape(64, 8 * BLOCKS)
    terms = exchange(terms.reshape(64, 1, 8 * BLOCKS), PLANE_GROUPS)
    terms = jnp.sum(terms, axis=0)
    whole = lax.all_to_all(
        jnp.broadcast_to(terms[None], (BLOCKS, 1, 8 * BLOCKS)), "dom", 0, 0, tiled=True
    )
    whole = whole.reshape(8, 2, 2, 4, 4, 2, BLOCKS).transpose(5, 2, 1, 0, 3, 4, 6)
    whole = whole.reshape(2, 2, 2, BLOCKS, BLOCKS)
    whole = jnp.where(core == 0, whole, whole[:, :, ::-1])
    whole = whole.reshape(2, 4 * BLOCKS, BLOCKS)
    rotated_near = rotate(rotation_near)
    lower = jnp.where(z_hi == 0, rotated_near, rotated_far)
    upper = jnp.where(z_hi == 0, rotated_far, rotated_near)
    rotated = jnp.concatenate([lower, upper], axis=0).reshape(1, BX, BY, BZ, width)
    return (rotated, whole[0], whole[1])


def solution(mesh):
    in_specs = (
        P("dom", None, None, None, "band"),
        P("dom", None, None, None),
        P(),
        P(None, "band"),
    )
    out_specs = (P("dom", None, None, None, "band"), P(None, "band"), P(None, "band"))
    return jax.shard_map(local, mesh=mesh, in_specs=in_specs, out_specs=out_specs, check_vma=False)
```

```python
import jax
import jax.numpy as jnp
from jax import lax
from jax.experimental import pallas as pl
from jax.experimental.pallas import tpu as pltpu
from jax.sharding import PartitionSpec as P

STENCIL = (
    -5369.0 / 1800.0,
    12.0 / 7.0,
    -15.0 / 56.0,
    10.0 / 189.0,
    -1.0 / 112.0,
    2.0 / 1925.0,
    -1.0 / 16632.0,
)
REACH = 6
KINETIC = -0.5 / 0.36
BX, BY, BZ = 8, 12, 16
CELLS = BX * BY * BZ
HALF = CELLS // 2
PX, PY, PZ = 4, 4, 8
BLOCKS = PX * PY * PZ
LANES = 128
TILES = CELLS // LANES
HALF_TILES = HALF // LANES
SENT = TILES + HALF_TILES

ORDER = [(ix * PY + iy) * PZ + iz for iz in range(PZ) for iy in range(PY) for ix in range(PX)]
STEP_X, STEP_Y, STEP_Z = 1, PX, PX * PY


def flat(band, dom):
    return band * BLOCKS + dom


def chip(y, x, z):
    return (y * 4 + x) * 4 + z


CORE_GROUPS = [[flat(2 * h + c, d) for d in ORDER for h in range(2)] for c in range(2)]
PLANE_GROUPS = [
    [flat(2 * h + c, chip(y, x, z)) for z in range(4) for y in range(8) for h in range(2)]
    for c in range(2)
    for x in range(4)
]
CORE_SWAP = [(0, 1), (1, 0), (2, 3), (3, 2)]
Z_SWAP = [(0, 2), (2, 0), (1, 3), (3, 1)]
Z_MIRROR = [
    (flat(b, chip(y, x, z)), flat(b ^ 2, chip(y, x, 3 - z)))
    for b in range(4)
    for y in range(8)
    for x in range(4)
    for z in range(4)
]


def exchange(x, groups):
    return lax.all_to_all(x, ("band", "dom"), 0, 0, tiled=True, axis_index_groups=groups)


OX, OY, OZ = REACH, REACH, 8
EXT = (BX + 2 * REACH, BY + 2 * REACH, BZ + 16, LANES)


def pack_kernel(core_ref, orbitals_ref, potential_ref, out_ref):
    for t in range(TILES):
        tile = orbitals_ref[t * LANES : (t + 1) * LANES]
        out_ref[pl.ds(t, BLOCKS, stride=SENT), :] = jnp.transpose(tile)
    for s in range(HALF_TILES):
        plane = potential_ref[core_ref[0] * HALF_TILES + s]
        row = jnp.concatenate([plane[i : i + 1] for i in range(BX)], axis=1)
        out_ref[pl.ds(TILES + s, BLOCKS, stride=SENT), :] = jnp.broadcast_to(row, (BLOCKS, LANES))


def packed(core, orbitals, potential):
    vmem = pl.BlockSpec(memory_space=pltpu.VMEM)
    return pl.pallas_call(
        pack_kernel,
        out_shape=jax.ShapeDtypeStruct((BLOCKS * SENT, LANES), jnp.float32),
        in_specs=[pl.BlockSpec(memory_space=pltpu.SMEM), vmem, vmem],
        out_specs=vmem,
        compiler_params=pltpu.CompilerParams(vmem_limit_bytes=16 * 1024 * 1024),
    )(core, orbitals, potential)


def split_kernel(got_ref, phi_ref, both_ref):
    for m in range(2):
        for h in range(2):
            for t in range(HALF_TILES):
                tile = got_ref[pl.ds(h * TILES + m * HALF_TILES + t, BLOCKS, stride=2 * TILES), :]
                cells = slice(t * LANES, (t + 1) * LANES)
                at = (2 * m + h) * BLOCKS
                both_ref[at : at + BLOCKS, cells] = tile
                if m == 0:
                    phi_ref[at : at + BLOCKS, cells] = tile


def split_fields(got):
    vmem = pl.BlockSpec(memory_space=pltpu.VMEM)
    return pl.pallas_call(
        split_kernel,
        out_shape=(
            jax.ShapeDtypeStruct((2 * BLOCKS, HALF), jnp.float32),
            jax.ShapeDtypeStruct((4 * BLOCKS, HALF), jnp.float32),
        ),
        in_specs=[vmem],
        out_specs=(vmem, vmem),
        compiler_params=pltpu.CompilerParams(vmem_limit_bytes=16 * 1024 * 1024),
    )(got)


def margins(ext):
    lane = lax.broadcasted_iota(jnp.int32, (8, LANES), 1)
    iz, iy, ix = lane // STEP_Z, lane // STEP_Y % PY, lane // STEP_X % PX
    masks = {0: (ix > 0, ix < PX - 1), 1: (iy > 0, iy < PY - 1), 2: (iz > 0, iz < PZ - 1)}
    steps = (STEP_X, STEP_Y, STEP_Z)

    def carry(dim, to_below, to_above, from_below, from_above):
        below, above = masks[dim]
        ext[to_below] = jnp.where(below, pltpu.roll(ext[from_below], steps[dim], 1), 0.0)
        ext[to_above] = jnp.where(above, pltpu.roll(ext[from_above], LANES - steps[dim], 1), 0.0)

    def at(x, y, z):
        return (x, y, slice(z, z + 8))

    for x in range(OX, OX + BX):
        for y in range(OY, OY + BY):
            carry(2, at(x, y, OZ - 8), at(x, y, OZ + BZ), at(x, y, OZ + BZ - 8), at(x, y, OZ))
        for y in range(OY):
            for z in range(OZ, OZ + BZ, 8):
                carry(1, at(x, y, z), at(x, y + OY + BY, z), at(x, y + BY, z), at(x, y + OY, z))
    for x in range(OX):
        for y in range(OY, OY + BY):
            for z in range(OZ, OZ + BZ, 8):
                carry(0, at(x, y, z), at(x + OX + BX, y, z), at(x + BX, y, z), at(x + OX, y, z))


YS = BY // 2


def own(ext, i, y0):
    return ext[i + OX, OY + y0 : OY + y0 + YS, OZ : OZ + BZ]


def set_own(ext, i, y0, value):
    ext[i + OX, OY + y0 : OY + y0 + YS, OZ : OZ + BZ] = value


def laplace(ext, i, y0):
    at, y, z = i + OX, OY + y0, OZ
    total = (3.0 * STENCIL[0]) * ext[at, y : y + YS, z : z + BZ]
    for k in range(1, REACH + 1):
        pair_x = ext[at - k, y : y + YS, z : z + BZ] + ext[at + k, y : y + YS, z : z + BZ]
        pair_y = ext[at, y - k : y - k + YS, z : z + BZ] + ext[at, y + k : y + k + YS, z : z + BZ]
        pair_z = ext[at, y : y + YS, z - k : z - k + BZ] + ext[at, y : y + YS, z + k : z + k + BZ]
        total = total + STENCIL[k] * ((pair_x + pair_y) + pair_z)
    return total


def laplace_kernel(got_ref, x_ref, lap_ref, pot_ref, ext):
    for q in range(TILES):
        tile = jnp.transpose(got_ref[pl.ds(q, BLOCKS, stride=SENT), :]).reshape(LANES // BZ, BZ, LANES)
        for r in range(LANES // BZ):
            row = q * (LANES // BZ) + r
            ext[OX + row // BY, OY + row % BY, OZ : OZ + BZ] = tile[r]
            x_ref[row // BY, row % BY] = tile[r]
    for s in range(HALF_TILES):
        tile = jnp.transpose(got_ref[pl.ds(TILES + s, BLOCKS, stride=SENT), :])
        pot_ref[:, s] = tile.reshape(BX, BZ, LANES)
    margins(ext)

    def body(i, carry):
        for y0 in range(0, BY, YS):
            lap_ref[i, y0 : y0 + YS] = laplace(ext, i, y0)
        return carry

    lax.fori_loop(0, BX, body, 0, unroll=True)


def filter_coefficients(bounds_ref):
    lowest, cutoff, highest = (jnp.full((1, LANES), bounds_ref[k], jnp.float32) for k in range(3))
    half_width = (highest - cutoff) / 2.0
    centre = (highest + cutoff) / 2.0
    s1 = half_width / (lowest - centre)
    tau = 2.0 / s1
    s2 = 1.0 / (tau - s1)
    s3 = 1.0 / (tau - s2)
    scales = (s1 / half_width, 2.0 * s2 / half_width, 2.0 * s3 / half_width)
    return centre, scales, (None, s1 * s2, s2 * s3)


def filter_kernel(core_ref, bounds_ref, x_ref, lap_ref, pot_own_ref, v_other_ref, out_ref, ea, eb, pot, img):
    shift, scales, backs = filter_coefficients(bounds_ref)
    second = core_ref[0] == 1
    for s in range(HALF_TILES):
        other = jnp.transpose(v_other_ref[pl.ds(s, BLOCKS, stride=HALF_TILES), :]).reshape(BX, BZ, LANES)
        mine = pot_own_ref[:, s]
        pot[:, s] = jnp.where(second, other, mine)
        pot[:, s + HALF_TILES] = jnp.where(second, mine, other)

    def image(total, centre, i, y0):
        return KINETIC * total + (pot[i, y0 : y0 + YS] - shift) * centre

    def first(i, carry):
        for y0 in range(0, BY, YS):
            total, centre = lap_ref[i, y0 : y0 + YS], x_ref[i, y0 : y0 + YS]
            set_own(eb, i, y0, scales[0] * image(total, centre, i, y0))
        return carry

    def next_field(i, carry):
        for y0 in range(0, BY, YS):
            new = scales[1] * image(laplace(eb, i, y0), own(eb, i, y0), i, y0)
            set_own(ea, i, y0, new - backs[1] * x_ref[i, y0 : y0 + YS])
        return carry

    def last_field(i, squares):
        for y0 in range(0, BY, YS):
            new = scales[2] * image(laplace(ea, i, y0), own(ea, i, y0), i, y0)
            new = new - backs[2] * own(eb, i, y0)
            set_own(eb, i, y0, new)
            squares = squares + jnp.sum(new * new, axis=0)
        return squares

    def image_field(i, carry):
        for y0 in range(0, BY, YS):
            centre = own(eb, i, y0)
            img[i, y0 : y0 + YS] = KINETIC * laplace(eb, i, y0) + pot[i, y0 : y0 + YS] * centre
        return carry

    lax.fori_loop(0, BX, first, 0, unroll=True)
    margins(eb)
    lax.fori_loop(0, BX, next_field, 0, unroll=True)
    margins(ea)
    squares = lax.fori_loop(0, BX, last_field, jnp.zeros((BZ, LANES), jnp.float32), unroll=True)
    margins(eb)
    lax.fori_loop(0, BX, image_field, 0, unroll=True)
    norm = jnp.sqrt(jnp.sum(squares, keepdims=True))
    for q in range(TILES):
        rows = [q * (LANES // BZ) + r for r in range(LANES // BZ)]
        at = q // HALF_TILES * TILES + q % HALF_TILES
        field = jnp.concatenate([eb[OX + r // BY, OY + r % BY, OZ : OZ + BZ] for r in rows], 0)
        out_ref[pl.ds(at, BLOCKS, stride=2 * TILES), :] = jnp.transpose(field / norm)
        field = jnp.concatenate([img[r // BY, r % BY] for r in rows], 0)
        out_ref[pl.ds(at + HALF_TILES, BLOCKS, stride=2 * TILES), :] = jnp.transpose(field / norm)


FIELD = (BX, BY, BZ, LANES)


def first_laplace(got):
    vmem = pl.BlockSpec(memory_space=pltpu.VMEM)
    return pl.pallas_call(
        laplace_kernel,
        out_shape=(
            jax.ShapeDtypeStruct(FIELD, jnp.float32),
            jax.ShapeDtypeStruct(FIELD, jnp.float32),
            jax.ShapeDtypeStruct((BX, HALF_TILES, BZ, LANES), jnp.float32),
        ),
        in_specs=[vmem],
        out_specs=(vmem, vmem, vmem),
        scratch_shapes=[pltpu.VMEM(EXT, jnp.float32)],
        compiler_params=pltpu.CompilerParams(vmem_limit_bytes=24 * 1024 * 1024),
        cost_estimate=pl.CostEstimate(flops=20_000_000, bytes_accessed=150_000_000, transcendentals=0),
    )(got)


def filtered_fields(core, bounds, x, lap, pot_own, v_other):
    vmem = pl.BlockSpec(memory_space=pltpu.VMEM)
    return pl.pallas_call(
        filter_kernel,
        out_shape=jax.ShapeDtypeStruct((BLOCKS * 2 * TILES, LANES), jnp.float32),
        in_specs=[pl.BlockSpec(memory_space=pltpu.SMEM)] * 2 + [vmem] * 4,
        out_specs=vmem,
        scratch_shapes=[
            pltpu.VMEM(EXT, jnp.float32),
            pltpu.VMEM(EXT, jnp.float32),
            pltpu.VMEM(FIELD, jnp.float32),
            pltpu.VMEM(FIELD, jnp.float32),
        ],
        compiler_params=pltpu.CompilerParams(vmem_limit_bytes=36 * 1024 * 1024),
        cost_estimate=pl.CostEstimate(flops=60_000_000, bytes_accessed=40_000_000, transcendentals=0),
    )(core, bounds, x, lap, pot_own, v_other)


def contract(left, right, dims):
    return lax.dot_general(
        left,
        right,
        (dims, ((), ())),
        precision=lax.Precision.HIGH,
        preferred_element_type=jnp.float32,
    )


def local(orbitals, potential, bounds, rotation):
    width = rotation.shape[1]
    band = lax.axis_index("band")
    z_hi, core = band >> 1, band & 1
    here = core.reshape(1)

    sent = packed(here, orbitals.reshape(CELLS, width), potential[0].transpose(1, 0, 2))
    got = lax.all_to_all(
        sent.reshape(BLOCKS, 1, SENT * LANES), "dom", 0, 0, tiled=True, axis_index_groups=[ORDER]
    )
    rotation_far = lax.ppermute(rotation, ("band", "dom"), Z_MIRROR)
    got, rotation_far = lax.optimization_barrier((got, rotation_far))
    v_other = lax.ppermute(got[:, :, CELLS:], "band", CORE_SWAP)
    x, lap, pot_own = first_laplace(got.reshape(BLOCKS * SENT, LANES))
    images = filtered_fields(
        here, bounds, x, lap, pot_own, v_other.reshape(BLOCKS * HALF_TILES, LANES)
    )

    spot = lax.axis_index("dom")
    got = exchange(images.reshape(2 * BLOCKS, 1, CELLS), CORE_GROUPS)
    got, rotation_near, rotation_far = lax.optimization_barrier((got, rotation, rotation_far))
    phi, both = split_fields(got.reshape(2 * BLOCKS * TILES, LANES))
    phi_other = lax.ppermute(phi, "band", CORE_SWAP)
    gram = jnp.concatenate(
        [contract(phi, both, ((1,), (1,))), contract(phi_other, both, ((1,), (1,)))], axis=0
    )

    def by_core(weights):
        weights = weights.reshape(2, 2, BLOCKS, width)
        swapped = jnp.where(core == 0, weights, weights[:, ::-1])
        return swapped.transpose(1, 0, 2, 3).reshape(4 * BLOCKS, width)

    def rotate(weights):
        weights = by_core(weights)
        return contract(phi, weights[: 2 * BLOCKS], ((0,), (0,))) + contract(
            phi_other, weights[2 * BLOCKS :], ((0,), (0,))
        )

    rotated_far = lax.ppermute(rotate(rotation_far), "band", Z_SWAP)

    gram = gram.reshape(4, BLOCKS, 4 * BLOCKS)
    place = ((spot >> 2) & 3).astype(jnp.uint32)
    pieces = [lax.dynamic_index_in_dim(gram, (place + k) & 3, 0, keepdims=False) for k in range(4)]
    for k in (2, 1, 3):
        pairs = [
            (chip(y, x, z), chip(y, (x + k) % 4, z)) for y in range(8) for x in range(4) for z in range(4)
        ]
        pieces[k] = lax.ppermute(pieces[k], "dom", pairs)
    terms, rotated_far = lax.optimization_barrier((pieces, rotated_far))
    terms = (terms[0] + terms[1]) + (terms[2] + terms[3])
    terms = terms.reshape(32, 4, 2, 2, BLOCKS).transpose(0, 3, 1, 2, 4).reshape(64, 8 * BLOCKS)
    terms = exchange(terms.reshape(64, 1, 8 * BLOCKS), PLANE_GROUPS)
    terms = jnp.sum(terms, axis=0)
    whole = lax.all_to_all(
        jnp.broadcast_to(terms[None], (BLOCKS, 1, 8 * BLOCKS)), "dom", 0, 0, tiled=True
    )
    whole = whole.reshape(8, 2, 2, 4, 4, 2, BLOCKS).transpose(5, 2, 1, 3, 0, 4, 6)
    whole = whole.reshape(2, 2, 2, BLOCKS, BLOCKS)
    whole = jnp.where(core == 0, whole, whole[:, :, ::-1])
    whole = whole.reshape(2, 4 * BLOCKS, BLOCKS)
    rotated_near = rotate(rotation_near)
    lower = jnp.where(z_hi == 0, rotated_near, rotated_far)
    upper = jnp.where(z_hi == 0, rotated_far, rotated_near)
    rotated = jnp.concatenate([lower, upper], axis=0).reshape(1, BX, BY, BZ, width)
    return (rotated, whole[0], whole[1])


def solution(mesh):
    in_specs = (
        P("dom", None, None, None, "band"),
        P("dom", None, None, None),
        P(),
        P(None, "band"),
    )
    out_specs = (P("dom", None, None, None, "band"), P(None, "band"), P(None, "band"))
    return jax.shard_map(local, mesh=mesh, in_specs=in_specs, out_specs=out_specs, check_vma=False)
```
